32 devices in a mesh: gx: 4 (over z), gy: 4 (over y, x), gz: 2 (over core).
Axes of the slice: x: 2, y: 2, z: 4, core: 2. Of those that a mesh axis runs over, the one named last changes fastest.
Arguments:
- populations: float32 [19, 16, 32, 512], P(None, 'gz', 'gx', 'gy'), may hold values from 0.6 to 1.4
- solid_codes: int32 [16, 32, 512], P('gz', 'gx', 'gy'), may hold values from 0 to 8
- plane_offsets: int32 [2, 2], replicated, may hold values from 0 to 31
- plane_fractions: int32 [2, 2], replicated, may hold values from 0 to 63
Outputs:
- populations_next: float32 [19, 16, 32, 512], P(None, 'gz', 'gx', 'gy')
The draws below stay inside these ranges and needn't reach their ends.
All inputs are finite; a program needn't handle non-finite values.
Results may differ from the reference program's by a relative error of at most 0.0001.
Values sent between devices are 32-bit elements; how exact they have to be, the bound alone decides.
A program may use at most 64 MiB of HBM per device.

```python
import jax
import jax.numpy as jnp

Q = 19
CZ = 8
STEPS = 2
LEVELS = 8
FRAC_DEN = 64
NX = 32
NY = 512
NZ = 16
PLANES = 2
N_GZ = 2


def plant(drawn, key, smallest, high):
    longest = drawn.shape.index(max(drawn.shape))
    spots = []
    for shift in (0, 1):
        where = [jax.random.randint(jax.random.fold_in(key, axis), (), 0, length) for axis, length in enumerate(drawn.shape)]
        where[longest] = (where[longest] + shift) % drawn.shape[longest]
        spots.append(tuple(where))
    return drawn.at[spots[0]].set(smallest).at[spots[1]].set(high)


def shard_levels(own_key, dims, pieces, low, top_value):
    loudness = 1.0
    for axis_at, blocks in pieces:
        draws = jax.random.uniform(jax.random.fold_in(jax.random.fold_in(own_key, 6), axis_at), (blocks,), jnp.float32, low / len(pieces), top_value / len(pieces))
        loudness = loudness * jnp.repeat(jnp.exp(draws), dims[axis_at] // blocks).reshape((-1,) + (1,) * (len(dims) - 1 - axis_at))
    return loudness


def setup_inputs(seed: int = 0) -> dict:
    keys = jax.random.split(jax.random.key(seed), 5)
    return {
        "populations": jnp.clip(0.6 + 0.79999995 * jax.random.uniform(keys[0], (Q, NZ, NX, NY), jnp.float32) ** shard_levels(keys[0], (Q, NZ, NX, NY), ((1, 2), (2, 4), (3, 4)), -0.2, 0.2), 0.6, 1.4),
        "solid_codes": plant(jax.random.randint(keys[1], (NZ, NX, NY), 0, LEVELS + 1), jax.random.fold_in(keys[1], 1), 0, LEVELS).astype(jnp.int32),
        "plane_offsets": plant(jax.random.randint(keys[2], (STEPS, PLANES), 0, NX), jax.random.fold_in(keys[2], 1), 0, NX - 1).astype(jnp.int32),
        "plane_fractions": plant(jax.random.randint(keys[3], (STEPS, PLANES), 0, FRAC_DEN), jax.random.fold_in(keys[3], 1), 0, FRAC_DEN - 1).astype(jnp.int32),
    }


velocities = ((0, 0, 0), (1, 0, 0), (-1, 0, 0), (0, 1, 0), (0, -1, 0), (0, 0, 1), (0, 0, -1), (1, 1, 0), (-1, -1, 0), (1, -1, 0), (-1, 1, 0), (1, 0, 1), (-1, 0, -1), (1, 0, -1), (-1, 0, 1), (0, 1, 1), (0, -1, -1), (0, 1, -1), (0, -1, 1))
lattice_weights = (1.0 / 3.0,) + (1.0 / 18.0,) * 6 + (1.0 / 36.0,) * 12
opposite_index = (0, 2, 1, 4, 3, 6, 5, 8, 7, 10, 9, 12, 11, 14, 13, 16, 15, 18, 17)
relax_time = 0.9
rising = (5, 11, 14, 15, 18)
sinking = (6, 12, 13, 16, 17)


def velocity_sum(distribution, component):
    total = jnp.zeros_like(distribution[0])
    for popul_index in range(19):
        moving = velocities[popul_index][component]
        if moving == 1:
            total = total + distribution[popul_index]
        elif moving == -1:
            total = total - distribution[popul_index]
    return total


def collide(distribution, solid_codes):
    solid = solid_codes.astype(jnp.float32) / LEVELS
    density = jnp.sum(distribution, axis=0)
    speed_x = velocity_sum(distribution, 0) / density
    speed_y = velocity_sum(distribution, 1) / density
    speed_z = velocity_sum(distribution, 2) / density
    square = speed_x * speed_x + speed_y * speed_y + speed_z * speed_z
    outgoing = []
    for popul_index in range(19):
        move_x, move_y, move_z = velocities[popul_index]
        along = move_x * speed_x + move_y * speed_y + move_z * speed_z
        balance = lattice_weights[popul_index] * density * (1.0 + 3.0 * along + 4.5 * along * along - 1.5 * square)
        relaxed = distribution[popul_index] - (distribution[popul_index] - balance) / relax_time
        outgoing.append((1.0 - solid) * relaxed + solid * distribution[opposite_index[popul_index]])
    return jnp.stack(outgoing)


def forward_move(layer_in, offset_in, weight_in):
    return (1.0 - weight_in) * jnp.roll(layer_in, offset_in, axis=1) + weight_in * jnp.roll(layer_in, offset_in + 1, axis=1)


def backward_move(layer_in, offset_in, weight_in):
    return (1.0 - weight_in) * jnp.roll(layer_in, -offset_in, axis=1) + weight_in * jnp.roll(layer_in, -offset_in - 1, axis=1)


def advance(distribution, solid_codes, offsets, fractions):
    collided = collide(distribution, solid_codes)
    blocks = collided.reshape(19, N_GZ, CZ, NX, NY)
    fraction = fractions.astype(jnp.float32) / FRAC_DEN
    top_layers = jnp.stack([blocks[popul_index, :, CZ - 1] for popul_index in rising])
    bottoms = jnp.stack([blocks[popul_index, :, 0] for popul_index in sinking])
    next_offset = jnp.roll(offsets, -1)
    next_fraction = jnp.roll(fraction, -1)
    raised = jax.vmap(forward_move, in_axes=(1, 0, 0), out_axes=1)(top_layers, next_offset, next_fraction)
    lowered = jax.vmap(backward_move, in_axes=(1, 0, 0), out_axes=1)(bottoms, offsets, fraction)
    from_below = jnp.roll(raised, 1, axis=1)
    from_above = jnp.roll(lowered, -1, axis=1)
    arrived = []
    for popul_index in range(19):
        move_x, move_y, move_z = velocities[popul_index]
        middle = blocks[popul_index]
        if move_z == 1:
            source = jnp.concatenate([from_below[rising.index(popul_index)][:, None], middle[:, :CZ - 1]], axis=1)
        elif move_z == -1:
            source = jnp.concatenate([middle[:, 1:], from_above[sinking.index(popul_index)][:, None]], axis=1)
        else:
            source = middle
        arrived.append(jnp.roll(source, (move_x, move_y), axis=(2, 3)))
    return jnp.stack(arrived).reshape(19, NZ, NX, NY)


def reference(populations, solid_codes, plane_offsets, plane_fractions):
    weights = jnp.asarray(lattice_weights, jnp.float32)[:, None, None, None]
    distribution = populations * weights
    for step_index in range(STEPS):
        distribution = advance(distribution, solid_codes, plane_offsets[step_index], plane_fractions[step_index])
    return distribution / weights
```

```python
import functools

import jax
import jax.numpy as jnp
from jax import lax
from jax.experimental import pallas as pl
from jax.experimental.pallas import tpu as pltpu
from jax.sharding import PartitionSpec as P

LEVELS = 8
FRAC_DEN = 64
MESH = pl.DeviceIdType.MESH

velocities = (
    (0, 0, 0),
    (1, 0, 0),
    (-1, 0, 0),
    (0, 1, 0),
    (0, -1, 0),
    (0, 0, 1),
    (0, 0, -1),
    (1, 1, 0),
    (-1, -1, 0),
    (1, -1, 0),
    (-1, 1, 0),
    (1, 0, 1),
    (-1, 0, -1),
    (1, 0, -1),
    (-1, 0, 1),
    (0, 1, 1),
    (0, -1, -1),
    (0, 1, -1),
    (0, -1, 1),
)
relax_time = 0.9
rising = (5, 11, 14, 15, 18)
sinking = (6, 12, 13, 16, 17)
x_movers = ((1, 7, 9, 11, 13), (2, 8, 10, 12, 14))
y_movers = ((3, 7, 10, 15, 17), (4, 8, 9, 16, 18))
corners = ((1, 1), (-1, -1), (1, -1), (-1, 1))


def side_of(move):
    return 0 if move > 0 else 1


def collide(pops, codes):
    solid = codes.astype(jnp.float32) * (1.0 / LEVELS)
    sums, diffs = {}, {}
    for i in range(1, 19, 2):
        sums[i] = pops[i] + pops[i + 1]
        diffs[i] = pops[i] - pops[i + 1]
    axis_sum = sums[1] + sums[3] + sums[5]
    diag_sum = (sums[7] + sums[9]) + (sums[11] + sums[13]) + (sums[15] + sums[17])
    density = pops[0] * (1.0 / 3.0) + axis_sum * (1.0 / 18.0) + diag_sum * (1.0 / 36.0)
    flow_x = diffs[1] * 2.0 + ((diffs[7] + diffs[9]) + (diffs[11] + diffs[13]))
    flow_y = diffs[3] * 2.0 + ((diffs[7] - diffs[9]) + (diffs[15] + diffs[17]))
    flow_z = diffs[5] * 2.0 + ((diffs[11] - diffs[13]) + (diffs[15] - diffs[17]))
    inverse = (1.0 / 36.0) / density
    ux, uy, uz = flow_x * inverse, flow_y * inverse, flow_z * inverse
    fluid = 1.0 - solid
    gain = density * fluid * (1.0 / relax_time)
    keep = fluid * (1.0 - 1.0 / relax_time)
    even = 0.5 * (keep + solid)
    odd = 0.5 * (keep - solid)
    rest = gain * (1.0 - 1.5 * (ux * ux + uy * uy + uz * uz))
    gain3, gain45 = gain * 3.0, gain * 4.5
    out = [None] * 19
    out[0] = (keep + solid) * pops[0] + rest
    along = {
        1: ux, 3: uy, 5: uz, 7: ux + uy, 9: ux - uy, 11: ux + uz, 13: ux - uz, 15: uy + uz, 17: uy - uz,
    }
    for i, a in along.items():
        part_even = even * sums[i] + (rest + gain45 * (a * a))
        part_odd = odd * diffs[i] + gain3 * a
        out[i] = part_even + part_odd
        out[i + 1] = part_even - part_odd
    return out


def kernel(
    sizes, off, frac, pops, codes, out,
    post, s_strip, s_row, s_col, s_corner, r_row, r_col, r_corner, send_sem, recv_sem, *gathers
):
    n_gx, n_gy, n_gz, steps = sizes
    r_strip, r_edge = gathers[:steps], gathers[steps:]
    layers, rows, cols = codes.shape
    length = n_gx * rows
    top = layers - 1
    gx, gy, gz = lax.axis_index("gx"), lax.axis_index("gy"), lax.axis_index("gz")
    merged = n_gz == 2
    z_moves = (1,) if merged else (1, -1)

    def peer(move):
        dx, dy, dz = move
        return (
            lax.rem(gx + (dx + n_gx), n_gx),
            lax.rem(gy + (dy + n_gy), n_gy),
            lax.rem(gz + (dz + n_gz), n_gz),
        )

    def messages(step):
        found = []
        for dz in z_moves:
            for k in range(n_gx):
                if merged:
                    src = s_strip.at[step]
                    dst = lambda at: r_strip[step].at[:, :, pl.ds(pl.multiple_of(at * rows, rows), rows), :]
                else:
                    src = s_strip.at[step, side_of(dz)]
                    dst = lambda at, d=side_of(dz): r_strip[step].at[
                        d, :, pl.ds(pl.multiple_of(at * rows, rows), rows), :
                    ]
                found.append(("strip", (k, 0, dz), src, dst))
        for dx in (1, -1):
            d = side_of(dx)
            found.append(("near", (dx, 0, 0), s_row.at[step, d], lambda at, d=d: r_row.at[step, d]))
        for dy in (1, -1):
            d = side_of(dy)
            found.append(("near", (0, dy, 0), s_col.at[step, d], lambda at, d=d: r_col.at[step, d]))
        for c, (dx, dy) in enumerate(corners):
            found.append(
                ("near", (dx, dy, 0), s_corner.at[step, c], lambda at, c=c: r_corner.at[step, c])
            )
        for zi, dz in enumerate(z_moves):
            for dy in (1, -1):
                d = side_of(dy)
                for k in range(n_gx):
                    found.append(
                        (
                            "edge",
                            (k, dy, dz),
                            s_col.at[step, d],
                            lambda at, zi=zi, d=d: r_edge[step].at[
                                zi, d, pl.ds(pl.multiple_of(at * rows, rows), rows), :
                            ],
                        )
                    )
        return found

    def copy_of(step, number, entry, incoming):
        group, move, src, dst = entry
        at = lax.rem(gx - move[0] + n_gx, n_gx) if incoming else gx
        return pltpu.make_async_remote_copy(
            src_ref=src,
            dst_ref=dst(at),
            send_sem=send_sem.at[step, number],
            recv_sem=recv_sem.at[step, number],
            device_id=peer(move),
            device_id_type=MESH,
        )

    def start(step, group):
        for number, entry in enumerate(messages(step)):
            if entry[0] == group:
                copy_of(step, number, entry, False).start()

    def arrive(step, group):
        for number, entry in enumerate(messages(step)):
            if entry[0] == group:
                copy_of(step, number, entry, True).wait_recv()

    def finish(step):
        for number, entry in enumerate(messages(step)):
            copy_of(step, number, entry, False).wait_send()

    moves = sorted({tuple(m % n for m, n in zip(entry[1], (n_gx, n_gy, n_gz))) for entry in messages(0)})
    barrier = pltpu.get_barrier_semaphore()
    for move in moves:
        pl.semaphore_signal(barrier, inc=1, device_id=peer(move), device_id_type=MESH)

    lane = lax.broadcasted_iota(jnp.int32, (rows, cols), 1)
    sub = lax.broadcasted_iota(jnp.int32, (rows, cols), 0)

    def to_lane(value, origin, target):
        return pltpu.roll(value, lax.rem(target - origin + 2 * cols, cols), 1)

    def publish(step, z, after, packed):
        for i in range(19):
            post[step, i, z] = after[i]
        for d in (0, 1):
            edge = rows - 1 if d == 0 else 0
            for j, i in enumerate(x_movers[d]):
                s_row[step, d, j, pl.ds(z, 1), :] = after[i][edge : edge + 1, :]
        result = []
        for d in (0, 1):
            value = packed[d]
            edge = cols - 1 if d == 0 else 0
            for j, i in enumerate(y_movers[d]):
                place = j * layers + z
                value = jnp.where(lane == place, to_lane(after[i], edge, place), value)
            result.append(value)
        return tuple(result)

    def publish_strips(step, z, after):
        if z == top:
            for j, i in enumerate(rising):
                s_strip[step, 0, j] = after[i]
        if z == 0:
            for j, i in enumerate(sinking):
                s_strip[step, 1, j] = after[i]

    def send_near(step, packed):
        for d in (0, 1):
            s_col[step, d] = packed[d]
        for c, (dx, dy) in enumerate(corners):
            edge = rows - 1 if dx > 0 else 0
            s_corner[step, c] = packed[side_of(dy)][edge : edge + 1, :]
        start(step, "near")
        start(step, "edge")

    def crossing(step, side, j, i):
        dx, dy, _ = velocities[i]
        if side == 0:
            plane = gz
            near = gx * rows - dx - off[step, plane]
            far = near - 1
        else:
            plane = lax.rem(gz + 1, n_gz)
            near = gx * rows - dx + off[step, plane]
            far = near + 1
        near = lax.rem(near + 2 * length, length)
        far = lax.rem(far + 2 * length, length)
        weight = frac[step, plane].astype(jnp.float32) * (1.0 / FRAC_DEN)
        value = (1.0 - weight) * r_strip[step][side, j, pl.ds(near, rows), :]
        value = value + weight * r_strip[step][side, j, pl.ds(far, rows), :]
        if dy == 0:
            return value
        d = side_of(dy)
        zi = 0 if merged else side
        halo = (1.0 - weight) * r_edge[step][zi, d, pl.ds(near, rows), :]
        halo = halo + weight * r_edge[step][zi, d, pl.ds(far, rows), :]
        target = 0 if dy > 0 else cols - 1
        place = y_movers[d].index(i) * layers + (top if side == 0 else 0)
        return jnp.where(lane == target, to_lane(halo, place, target), pltpu.roll(value, dy % cols, 1))

    def halo_columns(step):
        found = {}
        for dy in (1, -1):
            found[0, dy] = r_col[step, side_of(dy)]
        for c, (dx, dy) in enumerate(corners):
            edge = 0 if dx > 0 else rows - 1
            found[dx, dy] = jnp.where(
                sub == edge, r_corner[step, c], pltpu.roll(found[0, dy], dx % rows, 0)
            )
        return found

    def passed(step, z, halos, edge_layer):
        arrived = []
        for i in range(19):
            dx, dy, dz = velocities[i]
            if edge_layer == 0 and dz == 1:
                arrived.append(crossing(step, 0, rising.index(i), i))
                continue
            if edge_layer == top and dz == -1:
                arrived.append(crossing(step, 1, sinking.index(i), i))
                continue
            origin = z - dz
            value = post[step, i, origin]
            if dx:
                d = side_of(dx)
                edge = 0 if dx > 0 else rows - 1
                row = r_row[step, d, x_movers[d].index(i), pl.ds(origin, 1), :]
                value = jnp.where(sub == edge, row, pltpu.roll(value, dx % rows, 0))
            if dy:
                target = 0 if dy > 0 else cols - 1
                place = y_movers[side_of(dy)].index(i) * layers + origin
                value = jnp.where(
                    lane == target, to_lane(halos[dx, dy], place, target), pltpu.roll(value, dy % cols, 1)
                )
            arrived.append(value)
        return arrived

    def wrap_rows(step):
        for side in (0, 1):
            for j in range(5):
                r_strip[step][side, j, pl.ds(length, 2 * rows), :] = r_strip[step][side, j, pl.ds(0, 2 * rows), :]
        for zi in range(len(z_moves)):
            for d in (0, 1):
                r_edge[step][zi, d, pl.ds(length, 2 * rows), :] = r_edge[step][zi, d, pl.ds(0, 2 * rows), :]

    def inner(body, carry):
        per = 2
        whole = (layers - 2) // per

        def several(turn, carried):
            for k in range(per):
                carried = body(1 + turn * per + k, carried)
            return carried

        carry = lax.fori_loop(0, whole, several, carry)
        for z in range(1 + whole * per, top):
            carry = body(z, carry)
        return carry

    nothing = (jnp.zeros((rows, cols), jnp.float32),) * 2

    packed = nothing
    for z in (0, top):
        after = collide([pops[i, z] for i in range(19)], codes[z])
        publish_strips(0, z, after)
        packed = publish(0, z, after, packed)
    pl.semaphore_wait(barrier, len(moves))
    start(0, "strip")

    def first(z, packed):
        return publish(0, z, collide([pops[i, z] for i in range(19)], codes[z]), packed)

    send_near(0, inner(first, packed))

    for step in range(1, steps):
        arrive(step - 1, "near")
        halos = halo_columns(step - 1)

        def middle(z, packed, step=step, halos=halos):
            return publish(step, z, collide(passed(step - 1, z, halos, None), codes[z]), packed)

        packed = inner(middle, nothing)
        arrive(step - 1, "strip")
        arrive(step - 1, "edge")
        wrap_rows(step - 1)
        for z in (0, top):
            after = collide(passed(step - 1, z, halos, z), codes[z])
            publish_strips(step, z, after)
            packed = publish(step, z, after, packed)
        start(step, "strip")
        send_near(step, packed)

    arrive(steps - 1, "near")
    halos = halo_columns(steps - 1)

    def last(z, carry):
        for i, value in enumerate(passed(steps - 1, z, halos, None)):
            out[i, z] = value
        return carry

    inner(last, 0)
    arrive(steps - 1, "strip")
    arrive(steps - 1, "edge")
    wrap_rows(steps - 1)
    for z in (0, top):
        for i, value in enumerate(passed(steps - 1, z, halos, z)):
            out[i, z] = value
    for step in range(steps):
        finish(step)


def body(sizes, populations, solid_codes, plane_offsets, plane_fractions):
    n_gx, n_gy, n_gz = sizes
    _, layers, rows, cols = populations.shape
    steps = plane_offsets.shape[0]
    n_z = 1 if n_gz == 2 else 2
    gathered = n_gx * rows + 2 * rows
    n_messages = n_z * n_gx + 2 + 2 + 4 + n_z * 2 * n_gx
    f32 = jnp.float32
    return pl.pallas_call(
        functools.partial(kernel, (n_gx, n_gy, n_gz, steps)),
        out_shape=jax.ShapeDtypeStruct(populations.shape, f32),
        in_specs=[
            pl.BlockSpec(memory_space=pltpu.SMEM),
            pl.BlockSpec(memory_space=pltpu.SMEM),
            pl.BlockSpec(memory_space=pltpu.VMEM),
            pl.BlockSpec(memory_space=pltpu.VMEM),
        ],
        out_specs=pl.BlockSpec(memory_space=pltpu.VMEM),
        scratch_shapes=[
            pltpu.VMEM((steps, 19, layers, rows, cols), f32),
            pltpu.VMEM((steps, 2, 5, rows, cols), f32),
            pltpu.VMEM((steps, 2, 5, layers, cols), f32),
            pltpu.VMEM((steps, 2, rows, cols), f32),
            pltpu.VMEM((steps, 4, 1, cols), f32),
            pltpu.VMEM((steps, 2, 5, layers, cols), f32),
            pltpu.VMEM((steps, 2, rows, cols), f32),
            pltpu.VMEM((steps, 4, 1, cols), f32),
            pltpu.SemaphoreType.DMA((steps, n_messages)),
            pltpu.SemaphoreType.DMA((steps, n_messages)),
        ]
        + [pltpu.VMEM((2, 5, gathered, cols), f32)] * steps
        + [pltpu.VMEM((n_z, 2, gathered, cols), f32)] * steps,
        compiler_params=pltpu.CompilerParams(
            collective_id=0, has_side_effects=True, vmem_limit_bytes=32 * 1024 * 1024
        ),
    )(plane_offsets, plane_fractions, populations, solid_codes)


def solution(mesh):
    sizes = tuple(mesh.shape[name] for name in ("gx", "gy", "gz"))
    in_specs = (P(None, "gz", "gx", "gy"), P("gz", "gx", "gy"), P(), P())
    out_specs = P(None, "gz", "gx", "gy")
    return jax.shard_map(
        functools.partial(body, sizes), mesh=mesh, in_specs=in_specs, out_specs=out_specs, check_vma=False
    )
```

```python
import functools

import jax
import jax.numpy as jnp
from jax import lax
from jax.experimental import pallas as pl
from jax.experimental.pallas import tpu as pltpu
from jax.sharding import PartitionSpec as P

LEVELS = 8
FRAC_DEN = 64
MESH = pl.DeviceIdType.MESH

velocities = (
    (0, 0, 0),
    (1, 0, 0),
    (-1, 0, 0),
    (0, 1, 0),
    (0, -1, 0),
    (0, 0, 1),
    (0, 0, -1),
    (1, 1, 0),
    (-1, -1, 0),
    (1, -1, 0),
    (-1, 1, 0),
    (1, 0, 1),
    (-1, 0, -1),
    (1, 0, -1),
    (-1, 0, 1),
    (0, 1, 1),
    (0, -1, -1),
    (0, 1, -1),
    (0, -1, 1),
)
relax_time = 0.9
rising = (5, 11, 14, 15, 18)
sinking = (6, 12, 13, 16, 17)
x_movers = ((1, 7, 9, 11, 13), (2, 8, 10, 12, 14))
y_movers = ((3, 7, 10, 15, 17), (4, 8, 9, 16, 18))
corners = ((1, 1), (-1, -1), (1, -1), (-1, 1))


def side_of(move):
    return 0 if move > 0 else 1


def collide(pops, codes):
    solid = codes.astype(jnp.float32) * (1.0 / LEVELS)
    sums, diffs = {}, {}
    for i in range(1, 19, 2):
        sums[i] = pops[i] + pops[i + 1]
        diffs[i] = pops[i] - pops[i + 1]
    axis_sum = sums[1] + sums[3] + sums[5]
    diag_sum = (sums[7] + sums[9]) + (sums[11] + sums[13]) + (sums[15] + sums[17])
    density = pops[0] * (1.0 / 3.0) + axis_sum * (1.0 / 18.0) + diag_sum * (1.0 / 36.0)
    flow_x = diffs[1] * 2.0 + ((diffs[7] + diffs[9]) + (diffs[11] + diffs[13]))
    flow_y = diffs[3] * 2.0 + ((diffs[7] - diffs[9]) + (diffs[15] + diffs[17]))
    flow_z = diffs[5] * 2.0 + ((diffs[11] - diffs[13]) + (diffs[15] - diffs[17]))
    inverse = (1.0 / 36.0) / density
    ux, uy, uz = flow_x * inverse, flow_y * inverse, flow_z * inverse
    fluid = 1.0 - solid
    gain = density * fluid * (1.0 / relax_time)
    keep = fluid * (1.0 - 1.0 / relax_time)
    even = 0.5 * (keep + solid)
    odd = 0.5 * (keep - solid)
    rest = gain * (1.0 - 1.5 * (ux * ux + uy * uy + uz * uz))
    gain3, gain45 = gain * 3.0, gain * 4.5
    out = [None] * 19
    out[0] = (keep + solid) * pops[0] + rest
    along = {
        1: ux, 3: uy, 5: uz, 7: ux + uy, 9: ux - uy, 11: ux + uz, 13: ux - uz, 15: uy + uz, 17: uy - uz,
    }
    for i, a in along.items():
        part_even = even * sums[i] + (rest + gain45 * (a * a))
        part_odd = odd * diffs[i] + gain3 * a
        out[i] = part_even + part_odd
        out[i + 1] = part_even - part_odd
    return out


def kernel(
    sizes, off_in, frac_in, pops_in, codes_in, out_to,
    off, frac, pops, codes, out, load_sem, save_sem,
    post, s_strip, s_row, s_col, s_corner, s_edge, r_row, r_col, r_corner, r_edge, send_sem, recv_sem, *r_strip
):
    n_gx, n_gy, n_gz, steps = sizes
    layers, rows, cols = codes.shape
    length = n_gx * rows
    top = layers - 1
    gx, gy, gz = lax.axis_index("gx"), lax.axis_index("gy"), lax.axis_index("gz")
    merged = n_gz == 2
    z_moves = (1,) if merged else (1, -1)

    def peer(move):
        dx, dy, dz = move
        return (
            lax.rem(gx + (dx + n_gx), n_gx),
            lax.rem(gy + (dy + n_gy), n_gy),
            lax.rem(gz + (dz + n_gz), n_gz),
        )

    def messages(step):
        found = []
        for dz in z_moves:
            for k in range(n_gx):
                if merged:
                    src = s_strip.at[step]
                    dst = lambda at: r_strip[step].at[:, :, pl.ds(pl.multiple_of(at * rows, rows), rows), :]
                else:
                    src = s_strip.at[step, side_of(dz)]
                    dst = lambda at, d=side_of(dz): r_strip[step].at[
                        d, :, pl.ds(pl.multiple_of(at * rows, rows), rows), :
                    ]
                found.append(("strip", (k, 0, dz), src, dst))
        for dx in (1, -1):
            d = side_of(dx)
            found.append(("near", (dx, 0, 0), s_row.at[step, d], lambda at, d=d: r_row.at[step, d]))
        for dy in (1, -1):
            d = side_of(dy)
            found.append(("near", (0, dy, 0), s_col.at[step, d], lambda at, d=d: r_col.at[step, d]))
        for c, (dx, dy) in enumerate(corners):
            found.append(
                ("near", (dx, dy, 0), s_corner.at[step, c], lambda at, c=c: r_corner.at[step, c])
            )
        for zi, dz in enumerate(z_moves):
            for dy in (1, -1):
                d = side_of(dy)
                for k in range(n_gx):
                    found.append(
                        (
                            "edge",
                            (k, dy, dz),
                            s_edge.at[step, d],
                            lambda at, zi=zi, d=d: r_edge.at[step, zi, d, at],
                        )
                    )
        return found

    def copy_of(step, number, entry, incoming):
        group, move, src, dst = entry
        at = lax.rem(gx - move[0] + n_gx, n_gx) if incoming else gx
        return pltpu.make_async_remote_copy(
            src_ref=src,
            dst_ref=dst(at),
            send_sem=send_sem.at[step, number],
            recv_sem=recv_sem.at[step, number],
            device_id=peer(move),
            device_id_type=MESH,
        )

    def start(step, group):
        for number, entry in enumerate(messages(step)):
            if entry[0] == group:
                copy_of(step, number, entry, False).start()

    def arrive(step, group):
        for number, entry in enumerate(messages(step)):
            if entry[0] == group:
                copy_of(step, number, entry, True).wait_recv()

    def finish(step):
        for number, entry in enumerate(messages(step)):
            copy_of(step, number, entry, False).wait_send()

    inside = pl.ds(1, layers - 2)
    loads = [
        pltpu.make_async_copy(src, dst, load_sem.at[number])
        for number, (src, dst) in enumerate(
            (
                (codes_in, codes),
                (pops_in.at[:, 0], pops.at[:, 0]),
                (pops_in.at[:, top], pops.at[:, top]),
                (pops_in.at[:, inside], pops.at[:, inside]),
                (off_in, off),
                (frac_in, frac),
            )
        )
    ]
    for load in loads:
        load.start()

    moves = sorted({tuple(m % n for m, n in zip(entry[1], (n_gx, n_gy, n_gz))) for entry in messages(0)})
    barrier = pltpu.get_barrier_semaphore()
    for move in moves:
        pl.semaphore_signal(barrier, inc=1, device_id=peer(move), device_id_type=MESH)

    lane = lax.broadcasted_iota(jnp.int32, (rows, cols), 1)
    sub = lax.broadcasted_iota(jnp.int32, (rows, cols), 0)

    def to_lane(value, origin, target):
        return pltpu.roll(value, lax.rem(target - origin + 2 * cols, cols), 1)

    def publish(step, z, after, packed):
        for i in range(19):
            post[step, i, z] = after[i]
        for d in (0, 1):
            edge = rows - 1 if d == 0 else 0
            for j, i in enumerate(x_movers[d]):
                s_row[step, d, j, pl.ds(z, 1), :] = after[i][edge : edge + 1, :]
        result = []
        for d in (0, 1):
            value = packed[d]
            edge = cols - 1 if d == 0 else 0
            for j, i in enumerate(y_movers[d]):
                place = j * layers + z
                value = jnp.where(lane == place, to_lane(after[i], edge, place), value)
            result.append(value)
        return tuple(result)

    def publish_strips(step, bottom_after, top_after):
        for j, i in enumerate(rising):
            s_strip[step, 0, j] = top_after[i]
        for j, i in enumerate(sinking):
            s_strip[step, 1, j] = bottom_after[i]
        for d in (0, 1):
            dy = 1 if d == 0 else -1
            edge = cols - 1 if d == 0 else 0
            (up,) = [i for i in rising if velocities[i][1] == dy]
            (down,) = [i for i in sinking if velocities[i][1] == dy]
            place = gx * rows + sub
            spread = jnp.where(lane == place, top_after[up][:, edge : edge + 1], 0.0)
            spread = jnp.where(lane == place + length, bottom_after[down][:, edge : edge + 1], spread)
            s_edge[step, d] = jnp.sum(spread, axis=0, keepdims=True)

    def send(step, packed):
        for d in (0, 1):
            s_col[step, d] = packed[d]
        for c, (dx, dy) in enumerate(corners):
            edge = rows - 1 if dx > 0 else 0
            s_corner[step, c] = packed[side_of(dy)][edge : edge + 1, :]
        start(step, "near")
        start(step, "strip")
        start(step, "edge")

    def crossing(step, side, j, i):
        dx, dy, _ = velocities[i]
        if side == 0:
            plane = gz
            near = gx * rows - dx - off[step, plane]
            far = near - 1
        else:
            plane = lax.rem(gz + 1, n_gz)
            near = gx * rows - dx + off[step, plane]
            far = near + 1
        near = lax.rem(near + 2 * length, length)
        far = lax.rem(far + 2 * length, length)
        weight = frac[step, plane].astype(jnp.float32) * (1.0 / FRAC_DEN)
        value = (1.0 - weight) * r_strip[step][side, j, pl.ds(near, rows), :]
        value = value + weight * r_strip[step][side, j, pl.ds(far, rows), :]
        if dy == 0:
            return value
        d = side_of(dy)
        zi = 0 if merged else side
        gathered = r_edge[step, zi, d, 0]
        for k in range(1, n_gx):
            gathered = gathered + r_edge[step, zi, d, k]
        place_near, place_far = near + sub, far + sub
        place_near = jnp.where(place_near >= length, place_near - length, place_near) + side * length
        place_far = jnp.where(place_far >= length, place_far - length, place_far) + side * length
        picked = jnp.where(lane == place_near, 1.0 - weight, 0.0) + jnp.where(lane == place_far, weight, 0.0)
        halo = jnp.sum(gathered * picked, axis=1, keepdims=True)
        target = 0 if dy > 0 else cols - 1
        return jnp.where(lane == target, halo, pltpu.roll(value, dy % cols, 1))

    def halo_columns(step):
        found = {}
        for dy in (1, -1):
            found[0, dy] = r_col[step, side_of(dy)]
        for c, (dx, dy) in enumerate(corners):
            edge = 0 if dx > 0 else rows - 1
            found[dx, dy] = jnp.where(
                sub == edge, r_corner[step, c], pltpu.roll(found[0, dy], dx % rows, 0)
            )
        return found

    def passed(step, z, halos, edge_layer):
        arrived = []
        for i in range(19):
            dx, dy, dz = velocities[i]
            if edge_layer == 0 and dz == 1:
                arrived.append(crossing(step, 0, rising.index(i), i))
                continue
            if edge_layer == top and dz == -1:
                arrived.append(crossing(step, 1, sinking.index(i), i))
                continue
            origin = z - dz
            value = post[step, i, origin]
            if dx:
                d = side_of(dx)
                edge = 0 if dx > 0 else rows - 1
                row = r_row[step, d, x_movers[d].index(i), pl.ds(origin, 1), :]
                value = jnp.where(sub == edge, row, pltpu.roll(value, dx % rows, 0))
            if dy:
                target = 0 if dy > 0 else cols - 1
                place = y_movers[side_of(dy)].index(i) * layers + origin
                value = jnp.where(
                    lane == target, to_lane(halos[dx, dy], place, target), pltpu.roll(value, dy % cols, 1)
                )
            arrived.append(value)
        return arrived

    def wrap_rows(step):
        for side in (0, 1):
            for j in range(5):
                r_strip[step][side, j, pl.ds(length, 2 * rows), :] = r_strip[step][side, j, pl.ds(0, 2 * rows), :]

    def inner(body, carry):
        for z in range(1, top):
            carry = body(z, carry)
        return carry

    nothing = (jnp.zeros((rows, cols), jnp.float32),) * 2

    packed = nothing
    ends = {}
    loads[0].wait()
    for number, z in ((1, 0), (2, top)):
        loads[number].wait()
        ends[z] = collide([pops[i, z] for i in range(19)], codes[z])
        packed = publish(0, z, ends[z], packed)
    publish_strips(0, ends[0], ends[top])
    loads[3].wait()

    def first(z, packed):
        return publish(0, z, collide([pops[i, z] for i in range(19)], codes[z]), packed)

    packed = inner(first, packed)
    pl.semaphore_wait(barrier, len(moves))
    send(0, packed)
    loads[4].wait()
    loads[5].wait()

    for step in range(1, steps):
        arrive(step - 1, "near")
        halos = halo_columns(step - 1)

        def middle(z, packed, step=step, halos=halos):
            return publish(step, z, collide(passed(step - 1, z, halos, None), codes[z]), packed)

        packed = inner(middle, nothing)
        arrive(step - 1, "strip")
        arrive(step - 1, "edge")
        wrap_rows(step - 1)
        for z in (0, top):
            ends[z] = collide(passed(step - 1, z, halos, z), codes[z])
            packed = publish(step, z, ends[z], packed)
        publish_strips(step, ends[0], ends[top])
        send(step, packed)

    arrive(steps - 1, "near")
    halos = halo_columns(steps - 1)

    def last(z, carry):
        for i, value in enumerate(passed(steps - 1, z, halos, None)):
            out[i, z] = value
        return carry

    inner(last, 0)
    saves = [pltpu.make_async_copy(out.at[:, inside], out_to.at[:, inside], save_sem.at[0])]
    saves[0].start()
    arrive(steps - 1, "strip")
    arrive(steps - 1, "edge")
    wrap_rows(steps - 1)
    for z in (0, top):
        for i, value in enumerate(passed(steps - 1, z, halos, z)):
            out[i, z] = value
        saves.append(pltpu.make_async_copy(out.at[:, z], out_to.at[:, z], save_sem.at[len(saves)]))
        saves[-1].start()
    for step in range(steps):
        finish(step)
    for save in saves:
        save.wait()


def body(sizes, populations, solid_codes, plane_offsets, plane_fractions):
    n_gx, n_gy, n_gz = sizes
    _, layers, rows, cols = populations.shape
    steps = plane_offsets.shape[0]
    n_z = 1 if n_gz == 2 else 2
    gathered = n_gx * rows + 2 * rows
    n_messages = n_z * n_gx + 2 + 2 + 4 + n_z * 2 * n_gx
    f32 = jnp.float32
    return pl.pallas_call(
        functools.partial(kernel, (n_gx, n_gy, n_gz, steps)),
        out_shape=jax.ShapeDtypeStruct(populations.shape, f32),
        in_specs=[
            pl.BlockSpec(memory_space=pltpu.HBM),
            pl.BlockSpec(memory_space=pltpu.HBM),
            pl.BlockSpec(memory_space=pltpu.HBM),
            pl.BlockSpec(memory_space=pltpu.HBM),
        ],
        out_specs=pl.BlockSpec(memory_space=pltpu.HBM),
        scratch_shapes=[
            pltpu.SMEM(plane_offsets.shape, jnp.int32),
            pltpu.SMEM(plane_fractions.shape, jnp.int32),
            pltpu.VMEM(populations.shape, f32),
            pltpu.VMEM(solid_codes.shape, jnp.int32),
            pltpu.VMEM(populations.shape, f32),
            pltpu.SemaphoreType.DMA((6,)),
            pltpu.SemaphoreType.DMA((3,)),
            pltpu.VMEM((steps, 19, layers, rows, cols), f32),
            pltpu.VMEM((steps, 2, 5, rows, cols), f32),
            pltpu.VMEM((steps, 2, 5, layers, cols), f32),
            pltpu.VMEM((steps, 2, rows, cols), f32),
            pltpu.VMEM((steps, 4, 1, cols), f32),
            pltpu.VMEM((steps, 2, 1, cols), f32),
            pltpu.VMEM((steps, 2, 5, layers, cols), f32),
            pltpu.VMEM((steps, 2, rows, cols), f32),
            pltpu.VMEM((steps, 4, 1, cols), f32),
            pltpu.VMEM((steps, n_z, 2, n_gx, 1, cols), f32),
            pltpu.SemaphoreType.DMA((steps, n_messages)),
            pltpu.SemaphoreType.DMA((steps, n_messages)),
        ]
        + [pltpu.VMEM((2, 5, gathered, cols), f32)] * steps,
        compiler_params=pltpu.CompilerParams(
            collective_id=0, has_side_effects=True, vmem_limit_bytes=60 * 1024 * 1024
        ),
    )(plane_offsets, plane_fractions, populations, solid_codes)


def solution(mesh):
    sizes = tuple(mesh.shape[name] for name in ("gx", "gy", "gz"))
    in_specs = (P(None, "gz", "gx", "gy"), P("gz", "gx", "gy"), P(), P())
    out_specs = P(None, "gz", "gx", "gy")
    return jax.shard_map(
        functools.partial(body, sizes), mesh=mesh, in_specs=in_specs, out_specs=out_specs, check_vma=False
    )
```

```python
import functools

import jax
import jax.numpy as jnp
from jax import lax
from jax.experimental import pallas as pl
from jax.experimental.pallas import tpu as pltpu
from jax.sharding import PartitionSpec as P

LEVELS = 8
FRAC_DEN = 64
MESH = pl.DeviceIdType.MESH

velocities = (
    (0, 0, 0),
    (1, 0, 0),
    (-1, 0, 0),
    (0, 1, 0),
    (0, -1, 0),
    (0, 0, 1),
    (0, 0, -1),
    (1, 1, 0),
    (-1, -1, 0),
    (1, -1, 0),
    (-1, 1, 0),
    (1, 0, 1),
    (-1, 0, -1),
    (1, 0, -1),
    (-1, 0, 1),
    (0, 1, 1),
    (0, -1, -1),
    (0, 1, -1),
    (0, -1, 1),
)
relax_time = 0.9
rising = (5, 11, 14, 15, 18)
sinking = (6, 12, 13, 16, 17)
x_movers = ((1, 7, 9, 11, 13), (2, 8, 10, 12, 14))
y_movers = ((3, 7, 10, 15, 17), (4, 8, 9, 16, 18))
corners = ((1, 1), (-1, -1), (1, -1), (-1, 1))


def side_of(move):
    return 0 if move > 0 else 1


def collide(pops, codes):
    solid = codes.astype(jnp.float32) * (1.0 / LEVELS)
    sums, diffs = {}, {}
    for i in range(1, 19, 2):
        sums[i] = pops[i] + pops[i + 1]
        diffs[i] = pops[i] - pops[i + 1]
    axis_sum = sums[1] + sums[3] + sums[5]
    diag_sum = (sums[7] + sums[9]) + (sums[11] + sums[13]) + (sums[15] + sums[17])
    density = pops[0] * (1.0 / 3.0) + axis_sum * (1.0 / 18.0) + diag_sum * (1.0 / 36.0)
    flow_x = diffs[1] * 2.0 + ((diffs[7] + diffs[9]) + (diffs[11] + diffs[13]))
    flow_y = diffs[3] * 2.0 + ((diffs[7] - diffs[9]) + (diffs[15] + diffs[17]))
    flow_z = diffs[5] * 2.0 + ((diffs[11] - diffs[13]) + (diffs[15] - diffs[17]))
    inverse = (1.0 / 36.0) / density
    ux, uy, uz = flow_x * inverse, flow_y * inverse, flow_z * inverse
    fluid = 1.0 - solid
    gain = density * fluid * (1.0 / relax_time)
    keep = fluid * (1.0 - 1.0 / relax_time)
    even = 0.5 * (keep + solid)
    odd = 0.5 * (keep - solid)
    rest = gain * (1.0 - 1.5 * (ux * ux + uy * uy + uz * uz))
    gain3, gain45 = gain * 3.0, gain * 4.5
    out = [None] * 19
    out[0] = (keep + solid) * pops[0] + rest
    along = {
        1: ux, 3: uy, 5: uz, 7: ux + uy, 9: ux - uy, 11: ux + uz, 13: ux - uz, 15: uy + uz, 17: uy - uz,
    }
    for i, a in along.items():
        part_even = even * sums[i] + (rest + gain45 * (a * a))
        part_odd = odd * diffs[i] + gain3 * a
        out[i] = part_even + part_odd
        out[i + 1] = part_even - part_odd
    return out


def kernel(
    sizes, off_in, frac_in, pops_in, codes_in, out_to,
    off, frac, pops, codes, out, load_sem, save_sem,
    post, s_strip, s_inner, s_end, s_col, s_corner, s_edge,
    r_inner, r_end, r_col, r_corner, r_edge, send_sem, recv_sem, *gathers
):
    n_gx, n_gy, n_gz, steps = sizes
    r_strip = [gathers[2 * step : 2 * step + 2] for step in range(steps)]
    layers, rows, cols = codes.shape
    length = n_gx * rows
    top = layers - 1
    gx, gy, gz = lax.axis_index("gx"), lax.axis_index("gy"), lax.axis_index("gz")
    merged = n_gz == 2
    z_moves = (1,) if merged else (1, -1)

    def peer(move):
        dx, dy, dz = move
        return (
            lax.rem(gx + (dx + n_gx), n_gx),
            lax.rem(gy + (dy + n_gy), n_gy),
            lax.rem(gz + (dz + n_gz), n_gz),
        )

    def messages(step):
        found = []
        for side, dz in ((0, 1), (1, -1)):
            for k in range(n_gx):
                found.append(
                    (
                        ("rise", "sink")[side],
                        (k, 0, dz),
                        s_strip.at[step, side],
                        lambda at, side=side: r_strip[step][side].at[
                            :, pl.ds(pl.multiple_of(at * rows, rows), rows), :
                        ],
                    )
                )
        for dx in (1, -1):
            d = side_of(dx)
            found.append(("inner", (dx, 0, 0), s_inner.at[step, d], lambda at, d=d: r_inner.at[step, d]))
            found.append(("near", (dx, 0, 0), s_end.at[step, d], lambda at, d=d: r_end.at[step, d]))
        for dy in (1, -1):
            d = side_of(dy)
            found.append(("near", (0, dy, 0), s_col.at[step, d], lambda at, d=d: r_col.at[step, d]))
        for c, (dx, dy) in enumerate(corners):
            found.append(
                ("near", (dx, dy, 0), s_corner.at[step, c], lambda at, c=c: r_corner.at[step, c])
            )
        for zi, dz in enumerate(z_moves):
            for dy in (1, -1):
                d = side_of(dy)
                for k in range(n_gx):
                    found.append(
                        (
                            "edge",
                            (k, dy, dz),
                            s_edge.at[step, d],
                            lambda at, zi=zi, d=d: r_edge.at[step, zi, d, at],
                        )
                    )
        return found

    def copy_of(step, number, entry, incoming):
        group, move, src, dst = entry
        at = lax.rem(gx - move[0] + n_gx, n_gx) if incoming else gx
        return pltpu.make_async_remote_copy(
            src_ref=src,
            dst_ref=dst(at),
            send_sem=send_sem.at[step, number],
            recv_sem=recv_sem.at[step, number],
            device_id=peer(move),
            device_id_type=MESH,
        )

    def start(step, group):
        for number, entry in enumerate(messages(step)):
            if entry[0] == group:
                copy_of(step, number, entry, False).start()

    def arrive(step, group):
        for number, entry in enumerate(messages(step)):
            if entry[0] == group:
                copy_of(step, number, entry, True).wait_recv()

    def finish(step):
        for number, entry in enumerate(messages(step)):
            copy_of(step, number, entry, False).wait_send()

    inside = pl.ds(1, layers - 2)
    loads = [
        pltpu.make_async_copy(src, dst, load_sem.at[number])
        for number, (src, dst) in enumerate(
            (
                (codes_in, codes),
                (pops_in.at[:, 0], pops.at[:, 0]),
                (pops_in.at[:, top], pops.at[:, top]),
                (pops_in.at[:, inside], pops.at[:, inside]),
                (off_in, off),
                (frac_in, frac),
            )
        )
    ]
    for load in loads:
        load.start()

    moves = sorted({tuple(m % n for m, n in zip(entry[1], (n_gx, n_gy, n_gz))) for entry in messages(0)})
    barrier = pltpu.get_barrier_semaphore()
    for move in moves:
        pl.semaphore_signal(barrier, inc=1, device_id=peer(move), device_id_type=MESH)

    lane = lax.broadcasted_iota(jnp.int32, (rows, cols), 1)
    sub = lax.broadcasted_iota(jnp.int32, (rows, cols), 0)

    def to_lane(value, origin, target):
        return pltpu.roll(value, lax.rem(target - origin + 2 * cols, cols), 1)

    def publish(step, z, after, packed):
        for i in range(19):
            post[step, i, z] = after[i]
        for d in (0, 1):
            edge = rows - 1 if d == 0 else 0
            for j, i in enumerate(x_movers[d]):
                row = after[i][edge : edge + 1, :]
                if 0 < z < top:
                    place = (z - 1) * 5 + j
                    s_inner[step, d, place : place + 1, :] = row
                else:
                    place = j if z == 0 else 8 + j
                    s_end[step, d, place : place + 1, :] = row
        result = []
        for d in (0, 1):
            value = packed[d]
            edge = cols - 1 if d == 0 else 0
            for j, i in enumerate(y_movers[d]):
                place = j * layers + z
                value = jnp.where(lane == place, to_lane(after[i], edge, place), value)
            result.append(value)
        return tuple(result)

    def publish_strip(step, side, after):
        for j, i in enumerate((rising, sinking)[side]):
            s_strip[step, side, j] = after[i]

    def publish_edges(step, bottom_after, top_after):
        for d in (0, 1):
            dy = 1 if d == 0 else -1
            edge = cols - 1 if d == 0 else 0
            (up,) = [i for i in rising if velocities[i][1] == dy]
            (down,) = [i for i in sinking if velocities[i][1] == dy]
            place = gx * rows + sub
            spread = jnp.where(lane == place, top_after[up][:, edge : edge + 1], 0.0)
            spread = jnp.where(lane == place + length, bottom_after[down][:, edge : edge + 1], spread)
            s_edge[step, d] = jnp.sum(spread, axis=0, keepdims=True)

    def publish_columns(step, packed):
        for d in (0, 1):
            s_col[step, d] = packed[d]
        for c, (dx, dy) in enumerate(corners):
            edge = rows - 1 if dx > 0 else 0
            s_corner[step, c] = packed[side_of(dy)][edge : edge + 1, :]

    def crossing(step, side, j, i):
        dx, dy, _ = velocities[i]
        if side == 0:
            plane = gz
            near = gx * rows - dx - off[step, plane]
            far = near - 1
        else:
            plane = lax.rem(gz + 1, n_gz)
            near = gx * rows - dx + off[step, plane]
            far = near + 1
        near = lax.rem(near + 2 * length, length)
        far = lax.rem(far + 2 * length, length)
        weight = frac[step, plane].astype(jnp.float32) * (1.0 / FRAC_DEN)
        value = (1.0 - weight) * r_strip[step][side][j, pl.ds(near, rows), :]
        value = value + weight * r_strip[step][side][j, pl.ds(far, rows), :]
        if dy == 0:
            return value
        d = side_of(dy)
        zi = 0 if merged else side
        gathered = r_edge[step, zi, d, 0]
        for k in range(1, n_gx):
            gathered = gathered + r_edge[step, zi, d, k]
        place_near, place_far = near + sub, far + sub
        place_near = jnp.where(place_near >= length, place_near - length, place_near) + side * length
        place_far = jnp.where(place_far >= length, place_far - length, place_far) + side * length
        picked = jnp.where(lane == place_near, 1.0 - weight, 0.0) + jnp.where(lane == place_far, weight, 0.0)
        halo = jnp.sum(gathered * picked, axis=1, keepdims=True)
        target = 0 if dy > 0 else cols - 1
        return jnp.where(lane == target, halo, pltpu.roll(value, dy % cols, 1))

    def halo_columns(step):
        found = {}
        for dy in (1, -1):
            found[0, dy] = r_col[step, side_of(dy)]
        for c, (dx, dy) in enumerate(corners):
            edge = 0 if dx > 0 else rows - 1
            found[dx, dy] = jnp.where(
                sub == edge, r_corner[step, c], pltpu.roll(found[0, dy], dx % rows, 0)
            )
        return found

    def passed(step, z, halos, edge_layer):
        arrived = []
        for i in range(19):
            dx, dy, dz = velocities[i]
            if edge_layer == 0 and dz == 1:
                arrived.append(crossing(step, 0, rising.index(i), i))
                continue
            if edge_layer == top and dz == -1:
                arrived.append(crossing(step, 1, sinking.index(i), i))
                continue
            origin = z - dz
            value = post[step, i, origin]
            if dx:
                d = side_of(dx)
                edge = 0 if dx > 0 else rows - 1
                j = x_movers[d].index(i)
                if 0 < origin < top:
                    row = r_inner[step, d, pl.ds((origin - 1) * 5 + j, 1), :]
                else:
                    row = r_end[step, d, pl.ds(j if origin == 0 else 8 + j, 1), :]
                value = jnp.where(sub == edge, row, pltpu.roll(value, dx % rows, 0))
            if dy:
                target = 0 if dy > 0 else cols - 1
                place = y_movers[side_of(dy)].index(i) * layers + origin
                value = jnp.where(
                    lane == target, to_lane(halos[dx, dy], place, target), pltpu.roll(value, dy % cols, 1)
                )
            arrived.append(value)
        return arrived

    def wrap_rows(step, side):
        for j in range(5):
            r_strip[step][side][j, pl.ds(length, 2 * rows), :] = r_strip[step][side][j, pl.ds(0, 2 * rows), :]

    def inner(body, carry):
        for z in range(1, top):
            carry = body(z, carry)
        return carry

    nothing = (jnp.zeros((rows, cols), jnp.float32),) * 2

    packed = nothing
    ends = {}
    loads[0].wait()
    for number, z in ((1, 0), (2, top)):
        loads[number].wait()
        ends[z] = collide([pops[i, z] for i in range(19)], codes[z])
        packed = publish(0, z, ends[z], packed)
    publish_strip(0, 0, ends[top])
    publish_strip(0, 1, ends[0])
    publish_edges(0, ends[0], ends[top])
    pl.semaphore_wait(barrier, len(moves))
    start(0, "edge")
    start(0, "rise")
    loads[3].wait()

    def first(z, packed):
        return publish(0, z, collide([pops[i, z] for i in range(19)], codes[z]), packed)

    publish_columns(0, inner(first, packed))
    start(0, "inner")
    start(0, "near")
    start(0, "sink")
    loads[4].wait()
    loads[5].wait()

    for step in range(1, steps):
        arrive(step - 1, "inner")
        arrive(step - 1, "near")
        halos = halo_columns(step - 1)

        def middle(z, packed, step=step, halos=halos):
            return publish(step, z, collide(passed(step - 1, z, halos, None), codes[z]), packed)

        packed = inner(middle, nothing)
        start(step, "inner")
        arrive(step - 1, "edge")
        arrive(step - 1, "rise")
        wrap_rows(step - 1, 0)
        ends[0] = collide(passed(step - 1, 0, halos, 0), codes[0])
        publish_strip(step, 1, ends[0])
        start(step, "sink")
        packed = publish(step, 0, ends[0], packed)
        arrive(step - 1, "sink")
        wrap_rows(step - 1, 1)
        ends[top] = collide(passed(step - 1, top, halos, top), codes[top])
        publish_strip(step, 0, ends[top])
        publish_edges(step, ends[0], ends[top])
        start(step, "edge")
        start(step, "rise")
        publish_columns(step, publish(step, top, ends[top], packed))
        start(step, "near")

    step = steps - 1
    arrive(step, "inner")
    arrive(step, "near")
    halos = halo_columns(step)

    def last(z, carry):
        for i, value in enumerate(passed(step, z, halos, None)):
            out[i, z] = value
        return carry

    inner(last, 0)
    saves = [pltpu.make_async_copy(out.at[:, inside], out_to.at[:, inside], save_sem.at[0])]
    saves[0].start()
    arrive(step, "edge")
    for side, z in ((1, top), (0, 0)):
        arrive(step, ("rise", "sink")[side])
        wrap_rows(step, side)
        for i, value in enumerate(passed(step, z, halos, z)):
            out[i, z] = value
        saves.append(pltpu.make_async_copy(out.at[:, z], out_to.at[:, z], save_sem.at[len(saves)]))
        saves[-1].start()
    for step in range(steps):
        finish(step)
    for save in saves:
        save.wait()


def hand_over(chunks, source, target, sem):
    count = source.shape[0]
    cuts = [count * c // chunks for c in range(chunks + 1)]
    copies = []
    for c in range(chunks):
        part = pl.ds(cuts[c], cuts[c + 1] - cuts[c])
        copies.append(pltpu.make_async_copy(source.at[part], target.at[part], sem.at[c]))
    for copy in copies:
        copy.start()
    for copy in copies:
        copy.wait()


def body(sizes, populations, solid_codes, plane_offsets, plane_fractions):
    n_gx, n_gy, n_gz = sizes
    _, layers, rows, cols = populations.shape
    steps = plane_offsets.shape[0]
    n_z = 1 if n_gz == 2 else 2
    gathered = n_gx * rows + 2 * rows
    n_messages = 2 * n_gx + 2 * 2 + 2 + 4 + n_z * 2 * n_gx
    inner_rows = -(-5 * (layers - 2) // 8) * 8
    f32 = jnp.float32
    moved = pl.pallas_call(
        functools.partial(kernel, (n_gx, n_gy, n_gz, steps)),
        out_shape=jax.ShapeDtypeStruct(populations.shape, f32),
        in_specs=[
            pl.BlockSpec(memory_space=pltpu.HBM),
            pl.BlockSpec(memory_space=pltpu.HBM),
            pl.BlockSpec(memory_space=pltpu.HBM),
            pl.BlockSpec(memory_space=pltpu.HBM),
        ],
        out_specs=pl.BlockSpec(memory_space=pltpu.HBM),
        scratch_shapes=[
            pltpu.SMEM(plane_offsets.shape, jnp.int32),
            pltpu.SMEM(plane_fractions.shape, jnp.int32),
            pltpu.VMEM(populations.shape, f32),
            pltpu.VMEM(solid_codes.shape, jnp.int32),
            pltpu.VMEM(populations.shape, f32),
            pltpu.SemaphoreType.DMA((6,)),
            pltpu.SemaphoreType.DMA((3,)),
            pltpu.VMEM((steps, 19, layers, rows, cols), f32),
            pltpu.VMEM((steps, 2, 5, rows, cols), f32),
            pltpu.VMEM((steps, 2, inner_rows, cols), f32),
            pltpu.VMEM((steps, 2, 16, cols), f32),
            pltpu.VMEM((steps, 2, rows, cols), f32),
            pltpu.VMEM((steps, 4, 1, cols), f32),
            pltpu.VMEM((steps, 2, 1, cols), f32),
            pltpu.VMEM((steps, 2, inner_rows, cols), f32),
            pltpu.VMEM((steps, 2, 16, cols), f32),
            pltpu.VMEM((steps, 2, rows, cols), f32),
            pltpu.VMEM((steps, 4, 1, cols), f32),
            pltpu.VMEM((steps, n_z, 2, n_gx, 1, cols), f32),
            pltpu.SemaphoreType.DMA((steps, n_messages)),
            pltpu.SemaphoreType.DMA((steps, n_messages)),
        ]
        + [pltpu.VMEM((5, gathered, cols), f32)] * (2 * steps),
        compiler_params=pltpu.CompilerParams(
            collective_id=0, has_side_effects=True, vmem_limit_bytes=60 * 1024 * 1024
        ),
    )(plane_offsets, plane_fractions, populations, solid_codes)
    chunks = 7
    return pl.pallas_call(
        functools.partial(hand_over, chunks),
        out_shape=jax.ShapeDtypeStruct(populations.shape, f32),
        in_specs=[pl.BlockSpec(memory_space=pltpu.HBM)],
        out_specs=pl.BlockSpec(memory_space=pltpu.HBM),
        scratch_shapes=[pltpu.SemaphoreType.DMA((chunks,))],
        compiler_params=pltpu.CompilerParams(vmem_limit_bytes=60 * 1024 * 1024),
    )(moved)


def solution(mesh):
    sizes = tuple(mesh.shape[name] for name in ("gx", "gy", "gz"))
    in_specs = (P(None, "gz", "gx", "gy"), P("gz", "gx", "gy"), P(), P())
    out_specs = P(None, "gz", "gx", "gy")
    return jax.shard_map(
        functools.partial(body, sizes), mesh=mesh, in_specs=in_specs, out_specs=out_specs, check_vma=False
    )
```

```python
import functools

import jax
import jax.numpy as jnp
from jax import lax
from jax.experimental import pallas as pl
from jax.experimental.pallas import tpu as pltpu
from jax.sharding import PartitionSpec as P

LEVELS = 8
FRAC_DEN = 64
MESH = pl.DeviceIdType.MESH

velocities = (
    (0, 0, 0),
    (1, 0, 0),
    (-1, 0, 0),
    (0, 1, 0),
    (0, -1, 0),
    (0, 0, 1),
    (0, 0, -1),
    (1, 1, 0),
    (-1, -1, 0),
    (1, -1, 0),
    (-1, 1, 0),
    (1, 0, 1),
    (-1, 0, -1),
    (1, 0, -1),
    (-1, 0, 1),
    (0, 1, 1),
    (0, -1, -1),
    (0, 1, -1),
    (0, -1, 1),
)
relax_time = 0.9
rising = (5, 11, 14, 15, 18)
sinking = (6, 12, 13, 16, 17)
x_movers = ((1, 7, 9, 11, 13), (2, 8, 10, 12, 14))
y_movers = ((3, 7, 10, 15, 17), (4, 8, 9, 16, 18))
x_bottom = ((1, 7, 9, 11), (2, 8, 10, 14))
x_top = ((1, 7, 9, 13), (2, 8, 10, 12))
corners = ((1, 1), (-1, -1), (1, -1), (-1, 1))


def side_of(move):
    return 0 if move > 0 else 1


def collide(pops, codes):
    solid = codes.astype(jnp.float32) * (1.0 / LEVELS)
    sums, diffs = {}, {}
    for i in range(1, 19, 2):
        sums[i] = pops[i] + pops[i + 1]
        diffs[i] = pops[i] - pops[i + 1]
    axis_sum = sums[1] + sums[3] + sums[5]
    diag_sum = (sums[7] + sums[9]) + (sums[11] + sums[13]) + (sums[15] + sums[17])
    density = pops[0] * (1.0 / 3.0) + axis_sum * (1.0 / 18.0) + diag_sum * (1.0 / 36.0)
    flow_x = diffs[1] * 2.0 + ((diffs[7] + diffs[9]) + (diffs[11] + diffs[13]))
    flow_y = diffs[3] * 2.0 + ((diffs[7] - diffs[9]) + (diffs[15] + diffs[17]))
    flow_z = diffs[5] * 2.0 + ((diffs[11] - diffs[13]) + (diffs[15] - diffs[17]))
    inverse = (1.0 / 36.0) / density
    ux, uy, uz = flow_x * inverse, flow_y * inverse, flow_z * inverse
    fluid = 1.0 - solid
    gain = density * fluid * (1.0 / relax_time)
    keep = fluid * (1.0 - 1.0 / relax_time)
    even = 0.5 * (keep + solid)
    odd = 0.5 * (keep - solid)
    rest = gain * (1.0 - 1.5 * (ux * ux + uy * uy + uz * uz))
    gain3, gain45 = gain * 3.0, gain * 4.5
    out = [None] * 19
    out[0] = (keep + solid) * pops[0] + rest
    along = {
        1: ux, 3: uy, 5: uz, 7: ux + uy, 9: ux - uy, 11: ux + uz, 13: ux - uz, 15: uy + uz, 17: uy - uz,
    }
    for i, a in along.items():
        part_even = even * sums[i] + (rest + gain45 * (a * a))
        part_odd = odd * diffs[i] + gain3 * a
        out[i] = part_even + part_odd
        out[i + 1] = part_even - part_odd
    return out


def kernel(
    sizes, off_in, frac_in, pops_in, codes_in, out_to,
    off, frac, pops, codes, out, load_sem, save_sem,
    post, s_strip, s_inner, s_end, s_col, s_corner, s_edge,
    r_inner, r_end, r_col, r_corner, r_edge, send_sem, recv_sem, *gathers
):
    n_gx, n_gy, n_gz, steps = sizes
    r_strip = [gathers[2 * step : 2 * step + 2] for step in range(steps)]
    layers, rows, cols = codes.shape
    length = n_gx * rows
    top = layers - 1
    gx, gy, gz = lax.axis_index("gx"), lax.axis_index("gy"), lax.axis_index("gz")
    merged = n_gz == 2
    z_moves = (1,) if merged else (1, -1)

    def peer(move):
        dx, dy, dz = move
        return (
            lax.rem(gx + (dx + n_gx), n_gx),
            lax.rem(gy + (dy + n_gy), n_gy),
            lax.rem(gz + (dz + n_gz), n_gz),
        )

    def messages(step):
        found = []
        for side, dz in ((0, 1), (1, -1)):
            for k in range(n_gx):
                found.append(
                    (
                        ("rise", "sink")[side],
                        (k, 0, dz),
                        s_strip.at[step, side],
                        lambda at, side=side: r_strip[step][side].at[
                            :, pl.ds(pl.multiple_of(at * rows, rows), rows), :
                        ],
                    )
                )
        for dx in (1, -1):
            d = side_of(dx)
            found.append(("inner", (dx, 0, 0), s_inner.at[step, d], lambda at, d=d: r_inner.at[step, d]))
            found.append(("near", (dx, 0, 0), s_end.at[step, d], lambda at, d=d: r_end.at[step, d]))
        for dy in (1, -1):
            d = side_of(dy)
            found.append(("near", (0, dy, 0), s_col.at[step, d], lambda at, d=d: r_col.at[step, d]))
        for c, (dx, dy) in enumerate(corners):
            found.append(
                ("near", (dx, dy, 0), s_corner.at[step, c], lambda at, c=c: r_corner.at[step, c])
            )
        for zi, dz in enumerate(z_moves):
            for dy in (1, -1):
                d = side_of(dy)
                for k in range(n_gx):
                    found.append(
                        (
                            "edge",
                            (k, dy, dz),
                            s_edge.at[step, d],
                            lambda at, zi=zi, d=d: r_edge.at[step, zi, d, at],
                        )
                    )
        return found

    def copy_of(step, number, entry, incoming):
        group, move, src, dst = entry
        at = lax.rem(gx - move[0] + n_gx, n_gx) if incoming else gx
        return pltpu.make_async_remote_copy(
            src_ref=src,
            dst_ref=dst(at),
            send_sem=send_sem.at[step, number],
            recv_sem=recv_sem.at[step, number],
            device_id=peer(move),
            device_id_type=MESH,
        )

    def start(step, group):
        for number, entry in enumerate(messages(step)):
            if entry[0] == group:
                copy_of(step, number, entry, False).start()

    def arrive(step, group):
        for number, entry in enumerate(messages(step)):
            if entry[0] == group:
                copy_of(step, number, entry, True).wait_recv()

    def finish(step, groups):
        for number, entry in enumerate(messages(step)):
            if entry[0] in groups:
                copy_of(step, number, entry, False).wait_send()

    inside = pl.ds(1, layers - 2)
    loads = [
        pltpu.make_async_copy(src, dst, load_sem.at[number])
        for number, (src, dst) in enumerate(
            (
                (codes_in, codes),
                (pops_in.at[:, 0], pops.at[:, 0]),
                (pops_in.at[:, top], pops.at[:, top]),
                (pops_in.at[:, inside], pops.at[:, inside]),
                (off_in, off),
                (frac_in, frac),
            )
        )
    ]
    for load in loads:
        load.start()

    moves = sorted({tuple(m % n for m, n in zip(entry[1], (n_gx, n_gy, n_gz))) for entry in messages(0)})
    barrier = pltpu.get_barrier_semaphore()
    for move in moves:
        pl.semaphore_signal(barrier, inc=1, device_id=peer(move), device_id_type=MESH)

    lane = lax.broadcasted_iota(jnp.int32, (rows, cols), 1)
    sub = lax.broadcasted_iota(jnp.int32, (rows, cols), 0)

    def to_lane(value, origin, target):
        return pltpu.roll(value, lax.rem(target - origin + 2 * cols, cols), 1)

    def publish(step, z, after, packed):
        for i in range(19):
            post[step, i, z] = after[i]
        for d in (0, 1):
            edge = rows - 1 if d == 0 else 0
            if 0 < z < top:
                target, first_row, movers = s_inner, (z - 1) * 5, x_movers[d]
            elif z == 0:
                target, first_row, movers = s_end, 0, x_bottom[d]
            else:
                target, first_row, movers = s_end, 4, x_top[d]
            for j, i in enumerate(movers):
                place = first_row + j
                target[step, d, place : place + 1, :] = after[i][edge : edge + 1, :]
        result = []
        for d in (0, 1):
            value = packed[d]
            edge = cols - 1 if d == 0 else 0
            for j, i in enumerate(y_movers[d]):
                place = j * layers + z
                value = jnp.where(lane == place, to_lane(after[i], edge, place), value)
            result.append(value)
        return tuple(result)

    def publish_strip(step, side, after):
        for j, i in enumerate((rising, sinking)[side]):
            s_strip[step, side, j] = after[i]

    def publish_edges(step, bottom_after, top_after):
        for d in (0, 1):
            dy = 1 if d == 0 else -1
            edge = cols - 1 if d == 0 else 0
            (up,) = [i for i in rising if velocities[i][1] == dy]
            (down,) = [i for i in sinking if velocities[i][1] == dy]
            place = gx * rows + sub
            spread = jnp.where(lane == place, top_after[up][:, edge : edge + 1], 0.0)
            spread = jnp.where(lane == place + length, bottom_after[down][:, edge : edge + 1], spread)
            s_edge[step, d] = jnp.sum(spread, axis=0, keepdims=True)

    def publish_columns(step, packed):
        for d in (0, 1):
            s_col[step, d] = packed[d]
        for c, (dx, dy) in enumerate(corners):
            edge = rows - 1 if dx > 0 else 0
            s_corner[step, c] = packed[side_of(dy)][edge : edge + 1, :]

    def crossing(step, side, j, i):
        dx, dy, _ = velocities[i]
        if side == 0:
            plane = gz
            near = gx * rows - dx - off[step, plane]
            far = near - 1
        else:
            plane = lax.rem(gz + 1, n_gz)
            near = gx * rows - dx + off[step, plane]
            far = near + 1
        near = lax.rem(near + 2 * length, length)
        far = lax.rem(far + 2 * length, length)
        weight = frac[step, plane].astype(jnp.float32) * (1.0 / FRAC_DEN)
        value = (1.0 - weight) * r_strip[step][side][j, pl.ds(near, rows), :]
        value = value + weight * r_strip[step][side][j, pl.ds(far, rows), :]
        if dy == 0:
            return value
        d = side_of(dy)
        zi = 0 if merged else side
        gathered = r_edge[step, zi, d, 0]
        for k in range(1, n_gx):
            gathered = gathered + r_edge[step, zi, d, k]
        place_near, place_far = near + sub, far + sub
        place_near = jnp.where(place_near >= length, place_near - length, place_near) + side * length
        place_far = jnp.where(place_far >= length, place_far - length, place_far) + side * length
        picked = jnp.where(lane == place_near, 1.0 - weight, 0.0) + jnp.where(lane == place_far, weight, 0.0)
        halo = jnp.sum(gathered * picked, axis=1, keepdims=True)
        target = 0 if dy > 0 else cols - 1
        return jnp.where(lane == target, halo, pltpu.roll(value, dy % cols, 1))

    def halo_columns(step):
        found = {}
        for dy in (1, -1):
            found[0, dy] = r_col[step, side_of(dy)]
        for c, (dx, dy) in enumerate(corners):
            edge = 0 if dx > 0 else rows - 1
            found[dx, dy] = jnp.where(
                sub == edge, r_corner[step, c], pltpu.roll(found[0, dy], dx % rows, 0)
            )
        return found

    def passed(step, z, halos, edge_layer):
        arrived = []
        for i in range(19):
            dx, dy, dz = velocities[i]
            if edge_layer == 0 and dz == 1:
                arrived.append(crossing(step, 0, rising.index(i), i))
                continue
            if edge_layer == top and dz == -1:
                arrived.append(crossing(step, 1, sinking.index(i), i))
                continue
            origin = z - dz
            value = post[step, i, origin]
            if dx:
                d = side_of(dx)
                edge = 0 if dx > 0 else rows - 1
                if 0 < origin < top:
                    row = r_inner[step, d, pl.ds((origin - 1) * 5 + x_movers[d].index(i), 1), :]
                elif origin == 0:
                    row = r_end[step, d, pl.ds(x_bottom[d].index(i), 1), :]
                else:
                    row = r_end[step, d, pl.ds(4 + x_top[d].index(i), 1), :]
                value = jnp.where(sub == edge, row, pltpu.roll(value, dx % rows, 0))
            if dy:
                target = 0 if dy > 0 else cols - 1
                place = y_movers[side_of(dy)].index(i) * layers + origin
                value = jnp.where(
                    lane == target, to_lane(halos[dx, dy], place, target), pltpu.roll(value, dy % cols, 1)
                )
            arrived.append(value)
        return arrived

    def wrap_rows(step, side):
        for j in range(5):
            r_strip[step][side][j, pl.ds(length, 2 * rows), :] = r_strip[step][side][j, pl.ds(0, 2 * rows), :]

    def inner(body, carry):
        for z in range(1, top):
            carry = body(z, carry)
        return carry

    nothing = (jnp.zeros((rows, cols), jnp.float32),) * 2

    packed = nothing
    ends = {}
    loads[0].wait()
    for number, z in ((1, 0), (2, top)):
        loads[number].wait()
        ends[z] = collide([pops[i, z] for i in range(19)], codes[z])
        packed = publish(0, z, ends[z], packed)
    publish_strip(0, 0, ends[top])
    publish_strip(0, 1, ends[0])
    publish_edges(0, ends[0], ends[top])
    pl.semaphore_wait(barrier, len(moves))
    start(0, "edge")
    start(0, "rise")
    loads[3].wait()

    def first(z, packed):
        return publish(0, z, collide([pops[i, z] for i in range(19)], codes[z]), packed)

    publish_columns(0, inner(first, packed))
    start(0, "inner")
    start(0, "near")
    finish(0, ("rise",))
    start(0, "sink")
    loads[4].wait()
    loads[5].wait()

    for step in range(1, steps):
        arrive(step - 1, "inner")
        arrive(step - 1, "near")
        halos = halo_columns(step - 1)

        def middle(z, packed, step=step, halos=halos):
            return publish(step, z, collide(passed(step - 1, z, halos, None), codes[z]), packed)

        packed = inner(middle, nothing)
        start(step, "inner")
        arrive(step - 1, "edge")
        arrive(step - 1, "rise")
        wrap_rows(step - 1, 0)
        ends[0] = collide(passed(step - 1, 0, halos, 0), codes[0])
        publish_strip(step, 1, ends[0])
        start(step, "sink")
        packed = publish(step, 0, ends[0], packed)
        arrive(step - 1, "sink")
        wrap_rows(step - 1, 1)
        ends[top] = collide(passed(step - 1, top, halos, top), codes[top])
        publish_strip(step, 0, ends[top])
        publish_edges(step, ends[0], ends[top])
        start(step, "edge")
        start(step, "rise")
        publish_columns(step, publish(step, top, ends[top], packed))
        start(step, "near")

    step = steps - 1
    arrive(step, "inner")
    arrive(step, "near")
    halos = halo_columns(step)

    def last(z, carry):
        for i, value in enumerate(passed(step, z, halos, None)):
            out[i, z] = value
        return carry

    inner(last, 0)
    saves = [pltpu.make_async_copy(out.at[:, inside], out_to.at[:, inside], save_sem.at[0])]
    saves[0].start()
    arrive(step, "edge")
    for side, z in ((1, top), (0, 0)):
        arrive(step, ("rise", "sink")[side])
        wrap_rows(step, side)
        for i, value in enumerate(passed(step, z, halos, z)):
            out[i, z] = value
        saves.append(pltpu.make_async_copy(out.at[:, z], out_to.at[:, z], save_sem.at[len(saves)]))
        saves[-1].start()
    finish(0, ("sink", "inner", "near", "edge"))
    for step in range(1, steps):
        finish(step, ("rise", "sink", "inner", "near", "edge"))
    for save in saves:
        save.wait()


def hand_over(chunks, source, target, held, load_sem, save_sem):
    count = source.shape[0]
    cuts = [count * c // chunks for c in range(chunks + 1)]
    loads, saves = [], []
    for c in range(chunks):
        part = pl.ds(cuts[c], cuts[c + 1] - cuts[c])
        loads.append(pltpu.make_async_copy(source.at[part], held.at[part], load_sem.at[c]))
        saves.append(pltpu.make_async_copy(held.at[part], target.at[part], save_sem.at[c]))
    for load in loads:
        load.start()
    for load, save in zip(loads, saves):
        load.wait()
        save.start()
    for save in saves:
        save.wait()


def body(sizes, populations, solid_codes, plane_offsets, plane_fractions):
    n_gx, n_gy, n_gz = sizes
    _, layers, rows, cols = populations.shape
    steps = plane_offsets.shape[0]
    n_z = 1 if n_gz == 2 else 2
    gathered = n_gx * rows + 2 * rows
    n_messages = 2 * n_gx + 2 * 2 + 2 + 4 + n_z * 2 * n_gx
    inner_rows = -(-5 * (layers - 2) // 8) * 8
    f32 = jnp.float32
    moved = pl.pallas_call(
        functools.partial(kernel, (n_gx, n_gy, n_gz, steps)),
        out_shape=jax.ShapeDtypeStruct(populations.shape, f32),
        in_specs=[
            pl.BlockSpec(memory_space=pltpu.HBM),
            pl.BlockSpec(memory_space=pltpu.HBM),
            pl.BlockSpec(memory_space=pltpu.HBM),
            pl.BlockSpec(memory_space=pltpu.HBM),
        ],
        out_specs=pl.BlockSpec(memory_space=pltpu.HBM),
        scratch_shapes=[
            pltpu.SMEM(plane_offsets.shape, jnp.int32),
            pltpu.SMEM(plane_fractions.shape, jnp.int32),
            pltpu.VMEM(populations.shape, f32),
            pltpu.VMEM(solid_codes.shape, jnp.int32),
            pltpu.VMEM(populations.shape, f32),
            pltpu.SemaphoreType.DMA((6,)),
            pltpu.SemaphoreType.DMA((3,)),
            pltpu.VMEM((steps, 19, layers, rows, cols), f32),
            pltpu.VMEM((steps, 2, 5, rows, cols), f32),
            pltpu.VMEM((steps, 2, inner_rows, cols), f32),
            pltpu.VMEM((steps, 2, 8, cols), f32),
            pltpu.VMEM((steps, 2, rows, cols), f32),
            pltpu.VMEM((steps, 4, 1, cols), f32),
            pltpu.VMEM((steps, 2, 1, cols), f32),
            pltpu.VMEM((steps, 2, inner_rows, cols), f32),
            pltpu.VMEM((steps, 2, 8, cols), f32),
            pltpu.VMEM((steps, 2, rows, cols), f32),
            pltpu.VMEM((steps, 4, 1, cols), f32),
            pltpu.VMEM((steps, n_z, 2, n_gx, 1, cols), f32),
            pltpu.SemaphoreType.DMA((steps, n_messages)),
            pltpu.SemaphoreType.DMA((steps, n_messages)),
        ]
        + [pltpu.VMEM((5, gathered, cols), f32)] * (2 * steps),
        compiler_params=pltpu.CompilerParams(
            collective_id=0, has_side_effects=True, vmem_limit_bytes=60 * 1024 * 1024
        ),
    )(plane_offsets, plane_fractions, populations, solid_codes)
    chunks = 4
    return pl.pallas_call(
        functools.partial(hand_over, chunks),
        out_shape=jax.ShapeDtypeStruct(populations.shape, f32),
        in_specs=[pl.BlockSpec(memory_space=pltpu.HBM)],
        out_specs=pl.BlockSpec(memory_space=pltpu.HBM),
        scratch_shapes=[
            pltpu.VMEM(populations.shape, f32),
            pltpu.SemaphoreType.DMA((chunks,)),
            pltpu.SemaphoreType.DMA((chunks,)),
        ],
        compiler_params=pltpu.CompilerParams(vmem_limit_bytes=60 * 1024 * 1024),
    )(moved)


def solution(mesh):
    sizes = tuple(mesh.shape[name] for name in ("gx", "gy", "gz"))
    in_specs = (P(None, "gz", "gx", "gy"), P("gz", "gx", "gy"), P(), P())
    out_specs = P(None, "gz", "gx", "gy")
    return jax.shard_map(
        functools.partial(body, sizes), mesh=mesh, in_specs=in_specs, out_specs=out_specs, check_vma=False
    )
```

```python
import functools

import jax
import jax.numpy as jnp
from jax import lax
from jax.experimental import pallas as pl
from jax.experimental.pallas import tpu as pltpu
from jax.sharding import PartitionSpec as P

LEVELS = 8
FRAC_DEN = 64
MESH = pl.DeviceIdType.MESH

velocities = (
    (0, 0, 0),
    (1, 0, 0),
    (-1, 0, 0),
    (0, 1, 0),
    (0, -1, 0),
    (0, 0, 1),
    (0, 0, -1),
    (1, 1, 0),
    (-1, -1, 0),
    (1, -1, 0),
    (-1, 1, 0),
    (1, 0, 1),
    (-1, 0, -1),
    (1, 0, -1),
    (-1, 0, 1),
    (0, 1, 1),
    (0, -1, -1),
    (0, 1, -1),
    (0, -1, 1),
)
relax_time = 0.9
rising = (5, 11, 14, 15, 18)
sinking = (6, 12, 13, 16, 17)
x_movers = ((1, 7, 9, 11, 13), (2, 8, 10, 12, 14))
y_movers = ((3, 7, 10, 15, 17), (4, 8, 9, 16, 18))
x_bottom = ((1, 7, 9, 11), (2, 8, 10, 14))
x_top = ((1, 7, 9, 13), (2, 8, 10, 12))
corners = ((1, 1), (-1, -1), (1, -1), (-1, 1))


def side_of(move):
    return 0 if move > 0 else 1


def collide(pops, codes):
    solid = codes.astype(jnp.float32) * (1.0 / LEVELS)
    sums, diffs = {}, {}
    for i in range(1, 19, 2):
        sums[i] = pops[i] + pops[i + 1]
        diffs[i] = pops[i] - pops[i + 1]
    axis_sum = sums[1] + sums[3] + sums[5]
    diag_sum = (sums[7] + sums[9]) + (sums[11] + sums[13]) + (sums[15] + sums[17])
    density = pops[0] * (1.0 / 3.0) + axis_sum * (1.0 / 18.0) + diag_sum * (1.0 / 36.0)
    flow_x = diffs[1] * 2.0 + ((diffs[7] + diffs[9]) + (diffs[11] + diffs[13]))
    flow_y = diffs[3] * 2.0 + ((diffs[7] - diffs[9]) + (diffs[15] + diffs[17]))
    flow_z = diffs[5] * 2.0 + ((diffs[11] - diffs[13]) + (diffs[15] - diffs[17]))
    inverse = (1.0 / 36.0) / density
    ux, uy, uz = flow_x * inverse, flow_y * inverse, flow_z * inverse
    fluid = 1.0 - solid
    gain = density * fluid * (1.0 / relax_time)
    keep = fluid * (1.0 - 1.0 / relax_time)
    even = 0.5 * (keep + solid)
    odd = 0.5 * (keep - solid)
    rest = gain * (1.0 - 1.5 * (ux * ux + uy * uy + uz * uz))
    gain3, gain45 = gain * 3.0, gain * 4.5
    out = [None] * 19
    out[0] = (keep + solid) * pops[0] + rest
    along = {
        1: ux, 3: uy, 5: uz, 7: ux + uy, 9: ux - uy, 11: ux + uz, 13: ux - uz, 15: uy + uz, 17: uy - uz,
    }
    for i, a in along.items():
        part_even = even * sums[i] + (rest + gain45 * (a * a))
        part_odd = odd * diffs[i] + gain3 * a
        out[i] = part_even + part_odd
        out[i + 1] = part_even - part_odd
    return out


def kernel(
    sizes, pops, codes, out,
    table, table_sem,
    post, s_strip, s_inner, s_end, s_col, s_corner, s_edge,
    r_inner, r_end, r_col, r_corner, r_edge, send_sem, recv_sem, *gathers
):
    n_gx, n_gy, n_gz, steps = sizes
    r_strip = [gathers[2 * step : 2 * step + 2] for step in range(steps)]
    _, layers, rows, cols = pops.shape
    length = n_gx * rows
    top = layers - 1
    gx, gy, gz = lax.axis_index("gx"), lax.axis_index("gy"), lax.axis_index("gz")
    merged = n_gz == 2
    z_moves = (1,) if merged else (1, -1)

    def peer(move):
        dx, dy, dz = move
        return (
            lax.rem(gx + (dx + n_gx), n_gx),
            lax.rem(gy + (dy + n_gy), n_gy),
            lax.rem(gz + (dz + n_gz), n_gz),
        )

    def messages(step):
        found = []
        for side, dz in ((0, 1), (1, -1)):
            for k in range(n_gx):
                found.append(
                    (
                        ("rise", "sink")[side],
                        (k, 0, dz),
                        s_strip.at[step, side],
                        lambda at, side=side: r_strip[step][side].at[
                            :, pl.ds(pl.multiple_of(at * rows, rows), rows), :
                        ],
                    )
                )
        for dx in (1, -1):
            d = side_of(dx)
            found.append(("inner", (dx, 0, 0), s_inner.at[step, d], lambda at, d=d: r_inner.at[step, d]))
            found.append(("near", (dx, 0, 0), s_end.at[step, d], lambda at, d=d: r_end.at[step, d]))
        for dy in (1, -1):
            d = side_of(dy)
            found.append(("near", (0, dy, 0), s_col.at[step, d], lambda at, d=d: r_col.at[step, d]))
        for c, (dx, dy) in enumerate(corners):
            found.append(
                ("near", (dx, dy, 0), s_corner.at[step, c], lambda at, c=c: r_corner.at[step, c])
            )
        for zi, dz in enumerate(z_moves):
            for dy in (1, -1):
                d = side_of(dy)
                for k in range(n_gx):
                    found.append(
                        (
                            "edge",
                            (k, dy, dz),
                            s_edge.at[step, d],
                            lambda at, zi=zi, d=d: r_edge.at[step, zi, d, at],
                        )
                    )
        return found

    def copy_of(step, number, entry, incoming):
        group, move, src, dst = entry
        at = lax.rem(gx - move[0] + n_gx, n_gx) if incoming else gx
        return pltpu.make_async_remote_copy(
            src_ref=src,
            dst_ref=dst(at),
            send_sem=send_sem.at[step, number],
            recv_sem=recv_sem.at[step, number],
            device_id=peer(move),
            device_id_type=MESH,
        )

    def start(step, group):
        for number, entry in enumerate(messages(step)):
            if entry[0] == group:
                copy_of(step, number, entry, False).start()

    def arrive(step, group):
        for number, entry in enumerate(messages(step)):
            if entry[0] == group:
                copy_of(step, number, entry, True).wait_recv()

    def finish(step, groups):
        for number, entry in enumerate(messages(step)):
            if entry[0] in groups:
                copy_of(step, number, entry, False).wait_send()

    load_table = pltpu.make_async_copy(codes.at[pl.ds(layers * rows, rows)], table, table_sem)
    load_table.start()

    moves = sorted({tuple(m % n for m, n in zip(entry[1], (n_gx, n_gy, n_gz))) for entry in messages(0)})
    barrier = pltpu.get_barrier_semaphore()
    for move in moves:
        pl.semaphore_signal(barrier, inc=1, device_id=peer(move), device_id_type=MESH)

    lane = lax.broadcasted_iota(jnp.int32, (rows, cols), 1)
    sub = lax.broadcasted_iota(jnp.int32, (rows, cols), 0)

    def to_lane(value, origin, target):
        return pltpu.roll(value, lax.rem(target - origin + 2 * cols, cols), 1)

    def publish(step, z, after, packed):
        for i in range(19):
            post[step, i, z] = after[i]
        for d in (0, 1):
            edge = rows - 1 if d == 0 else 0
            if 0 < z < top:
                target, first_row, movers = s_inner, (z - 1) * 5, x_movers[d]
            elif z == 0:
                target, first_row, movers = s_end, 0, x_bottom[d]
            else:
                target, first_row, movers = s_end, 4, x_top[d]
            for j, i in enumerate(movers):
                place = first_row + j
                target[step, d, place : place + 1, :] = after[i][edge : edge + 1, :]
        result = []
        for d in (0, 1):
            value = packed[d]
            edge = cols - 1 if d == 0 else 0
            for j, i in enumerate(y_movers[d]):
                place = j * layers + z
                value = jnp.where(lane == place, to_lane(after[i], edge, place), value)
            result.append(value)
        return tuple(result)

    def publish_strip(step, side, after):
        for j, i in enumerate((rising, sinking)[side]):
            s_strip[step, side, j] = after[i]

    def publish_edges(step, bottom_after, top_after):
        for d in (0, 1):
            dy = 1 if d == 0 else -1
            edge = cols - 1 if d == 0 else 0
            (up,) = [i for i in rising if velocities[i][1] == dy]
            (down,) = [i for i in sinking if velocities[i][1] == dy]
            place = gx * rows + sub
            spread = jnp.where(lane == place, top_after[up][:, edge : edge + 1], 0.0)
            spread = jnp.where(lane == place + length, bottom_after[down][:, edge : edge + 1], spread)
            s_edge[step, d] = jnp.sum(spread, axis=0, keepdims=True)

    def publish_columns(step, packed):
        for d in (0, 1):
            s_col[step, d] = packed[d]
        for c, (dx, dy) in enumerate(corners):
            edge = rows - 1 if dx > 0 else 0
            s_corner[step, c] = packed[side_of(dy)][edge : edge + 1, :]

    def crossing(step, side, j, i):
        dx, dy, _ = velocities[i]
        if side == 0:
            plane = gz
            near = gx * rows - dx - table[step, plane]
            far = near - 1
        else:
            plane = lax.rem(gz + 1, n_gz)
            near = gx * rows - dx + table[step, plane]
            far = near + 1
        near = lax.rem(near + 2 * length, length)
        far = lax.rem(far + 2 * length, length)
        weight = table[steps + step, plane].astype(jnp.float32) * (1.0 / FRAC_DEN)
        value = (1.0 - weight) * r_strip[step][side][j, pl.ds(near, rows), :]
        value = value + weight * r_strip[step][side][j, pl.ds(far, rows), :]
        if dy == 0:
            return value
        d = side_of(dy)
        zi = 0 if merged else side
        gathered = r_edge[step, zi, d, 0]
        for k in range(1, n_gx):
            gathered = gathered + r_edge[step, zi, d, k]
        place_near, place_far = near + sub, far + sub
        place_near = jnp.where(place_near >= length, place_near - length, place_near) + side * length
        place_far = jnp.where(place_far >= length, place_far - length, place_far) + side * length
        picked = jnp.where(lane == place_near, 1.0 - weight, 0.0) + jnp.where(lane == place_far, weight, 0.0)
        halo = jnp.sum(gathered * picked, axis=1, keepdims=True)
        target = 0 if dy > 0 else cols - 1
        return jnp.where(lane == target, halo, pltpu.roll(value, dy % cols, 1))

    def halo_columns(step):
        found = {}
        for dy in (1, -1):
            found[0, dy] = r_col[step, side_of(dy)]
        for c, (dx, dy) in enumerate(corners):
            edge = 0 if dx > 0 else rows - 1
            found[dx, dy] = jnp.where(
                sub == edge, r_corner[step, c], pltpu.roll(found[0, dy], dx % rows, 0)
            )
        return found

    def passed(step, z, halos, edge_layer):
        arrived = []
        for i in range(19):
            dx, dy, dz = velocities[i]
            if edge_layer == 0 and dz == 1:
                arrived.append(crossing(step, 0, rising.index(i), i))
                continue
            if edge_layer == top and dz == -1:
                arrived.append(crossing(step, 1, sinking.index(i), i))
                continue
            origin = z - dz
            value = post[step, i, origin]
            if dx:
                d = side_of(dx)
                edge = 0 if dx > 0 else rows - 1
                if 0 < origin < top:
                    row = r_inner[step, d, pl.ds((origin - 1) * 5 + x_movers[d].index(i), 1), :]
                elif origin == 0:
                    row = r_end[step, d, pl.ds(x_bottom[d].index(i), 1), :]
                else:
                    row = r_end[step, d, pl.ds(4 + x_top[d].index(i), 1), :]
                value = jnp.where(sub == edge, row, pltpu.roll(value, dx % rows, 0))
            if dy:
                target = 0 if dy > 0 else cols - 1
                place = y_movers[side_of(dy)].index(i) * layers + origin
                value = jnp.where(
                    lane == target, to_lane(halos[dx, dy], place, target), pltpu.roll(value, dy % cols, 1)
                )
            arrived.append(value)
        return arrived

    def wrap_rows(step, side):
        for j in range(5):
            r_strip[step][side][j, pl.ds(length, 2 * rows), :] = r_strip[step][side][j, pl.ds(0, 2 * rows), :]

    def inner(body, carry):
        for z in range(1, top):
            carry = body(z, carry)
        return carry

    nothing = (jnp.zeros((rows, cols), jnp.float32),) * 2

    packed = nothing
    ends = {}
    for z in (0, top):
        ends[z] = collide([pops[i, z] for i in range(19)], codes[z * rows : (z + 1) * rows])
        packed = publish(0, z, ends[z], packed)
    publish_strip(0, 0, ends[top])
    publish_strip(0, 1, ends[0])
    publish_edges(0, ends[0], ends[top])
    pl.semaphore_wait(barrier, len(moves))
    start(0, "rise")
    start(0, "edge")

    def first(z, packed):
        return publish(0, z, collide([pops[i, z] for i in range(19)], codes[z * rows : (z + 1) * rows]), packed)

    publish_columns(0, inner(first, packed))
    start(0, "inner")
    start(0, "near")
    finish(0, ("rise",))
    start(0, "sink")
    load_table.wait()

    for step in range(1, steps):
        arrive(step - 1, "inner")
        arrive(step - 1, "near")
        halos = halo_columns(step - 1)

        def middle(z, packed, step=step, halos=halos):
            return publish(step, z, collide(passed(step - 1, z, halos, None), codes[z * rows : (z + 1) * rows]), packed)

        packed = inner(middle, nothing)
        start(step, "inner")
        arrive(step - 1, "edge")
        arrive(step - 1, "rise")
        wrap_rows(step - 1, 0)
        ends[0] = collide(passed(step - 1, 0, halos, 0), codes[:rows])
        publish_strip(step, 1, ends[0])
        start(step, "sink")
        packed = publish(step, 0, ends[0], packed)
        arrive(step - 1, "sink")
        wrap_rows(step - 1, 1)
        ends[top] = collide(passed(step - 1, top, halos, top), codes[top * rows : layers * rows])
        publish_strip(step, 0, ends[top])
        publish_edges(step, ends[0], ends[top])
        start(step, "edge")
        start(step, "rise")
        publish_columns(step, publish(step, top, ends[top], packed))
        start(step, "near")

    step = steps - 1
    arrive(step, "inner")
    arrive(step, "near")
    halos = halo_columns(step)

    def last(z, carry):
        for i, value in enumerate(passed(step, z, halos, None)):
            out[i, z] = value
        return carry

    inner(last, 0)
    arrive(step, "edge")
    for side, z in ((1, top), (0, 0)):
        arrive(step, ("rise", "sink")[side])
        wrap_rows(step, side)
        for i, value in enumerate(passed(step, z, halos, z)):
            out[i, z] = value
    finish(0, ("sink", "inner", "near", "edge"))
    for step in range(1, steps):
        finish(step, ("rise", "sink", "inner", "near", "edge"))


def body(sizes, populations, solid_codes, plane_offsets, plane_fractions):
    n_gx, n_gy, n_gz = sizes
    _, layers, rows, cols = populations.shape
    steps = plane_offsets.shape[0]
    n_z = 1 if n_gz == 2 else 2
    gathered = n_gx * rows + 2 * rows
    n_messages = 2 * n_gx + 2 * 2 + 2 + 4 + n_z * 2 * n_gx
    inner_rows = -(-5 * (layers - 2) // 8) * 8
    f32 = jnp.float32
    planes = plane_offsets.shape[1]
    beyond = cols - planes
    cells = layers * rows
    codes = jnp.pad(solid_codes.reshape(cells, cols), ((0, rows), (0, 0)))
    codes += jnp.pad(plane_offsets, ((cells, rows - steps), (0, beyond)))
    codes += jnp.pad(plane_fractions, ((cells + steps, rows - 2 * steps), (0, beyond)))
    return pl.pallas_call(
        functools.partial(kernel, (n_gx, n_gy, n_gz, steps)),
        out_shape=jax.ShapeDtypeStruct(populations.shape, f32),
        in_specs=[
            pl.BlockSpec(memory_space=pltpu.VMEM),
            pl.BlockSpec(memory_space=pltpu.VMEM),
        ],
        out_specs=pl.BlockSpec(memory_space=pltpu.VMEM),
        scratch_shapes=[
            pltpu.SMEM((rows, cols), jnp.int32),
            pltpu.SemaphoreType.DMA(()),
            pltpu.VMEM((steps, 19, layers, rows, cols), f32),
            pltpu.VMEM((steps, 2, 5, rows, cols), f32),
            pltpu.VMEM((steps, 2, inner_rows, cols), f32),
            pltpu.VMEM((steps, 2, 8, cols), f32),
            pltpu.VMEM((steps, 2, rows, cols), f32),
            pltpu.VMEM((steps, 4, 1, cols), f32),
            pltpu.VMEM((steps, 2, 1, cols), f32),
            pltpu.VMEM((steps, 2, inner_rows, cols), f32),
            pltpu.VMEM((steps, 2, 8, cols), f32),
            pltpu.VMEM((steps, 2, rows, cols), f32),
            pltpu.VMEM((steps, 4, 1, cols), f32),
            pltpu.VMEM((steps, n_z, 2, n_gx, 1, cols), f32),
            pltpu.SemaphoreType.DMA((steps, n_messages)),
            pltpu.SemaphoreType.DMA((steps, n_messages)),
        ]
        + [pltpu.VMEM((5, gathered, cols), f32)] * (2 * steps),
        compiler_params=pltpu.CompilerParams(
            collective_id=0, has_side_effects=True, vmem_limit_bytes=32 * 1024 * 1024
        ),
    )(populations, codes)


def solution(mesh):
    sizes = tuple(mesh.shape[name] for name in ("gx", "gy", "gz"))
    in_specs = (P(None, "gz", "gx", "gy"), P("gz", "gx", "gy"), P(), P())
    out_specs = P(None, "gz", "gx", "gy")
    return jax.shard_map(
        functools.partial(body, sizes), mesh=mesh, in_specs=in_specs, out_specs=out_specs, check_vma=False
    )
```

```python
import functools

import jax
import jax.numpy as jnp
from jax import lax
from jax.experimental import pallas as pl
from jax.experimental.pallas import tpu as pltpu
from jax.sharding import PartitionSpec as P

LEVELS = 8
FRAC_DEN = 64
MESH = pl.DeviceIdType.MESH

velocities = (
    (0, 0, 0),
    (1, 0, 0),
    (-1, 0, 0),
    (0, 1, 0),
    (0, -1, 0),
    (0, 0, 1),
    (0, 0, -1),
    (1, 1, 0),
    (-1, -1, 0),
    (1, -1, 0),
    (-1, 1, 0),
    (1, 0, 1),
    (-1, 0, -1),
    (1, 0, -1),
    (-1, 0, 1),
    (0, 1, 1),
    (0, -1, -1),
    (0, 1, -1),
    (0, -1, 1),
)
relax_time = 0.9
rising = (5, 11, 14, 15, 18)
sinking = (6, 12, 13, 16, 17)
x_movers = ((1, 7, 9, 11, 13), (2, 8, 10, 12, 14))
y_movers = ((3, 7, 10, 15, 17), (4, 8, 9, 16, 18))
x_bottom = ((1, 7, 9, 11), (2, 8, 10, 14))
x_top = ((1, 7, 9, 13), (2, 8, 10, 12))
corners = ((1, 1), (-1, -1), (1, -1), (-1, 1))


def side_of(move):
    return 0 if move > 0 else 1


def collide(pops, codes):
    solid = codes.astype(jnp.float32) * (1.0 / LEVELS)
    sums, diffs = {}, {}
    for i in range(1, 19, 2):
        sums[i] = pops[i] + pops[i + 1]
        diffs[i] = pops[i] - pops[i + 1]
    axis_sum = sums[1] + sums[3] + sums[5]
    diag_sum = (sums[7] + sums[9]) + (sums[11] + sums[13]) + (sums[15] + sums[17])
    density = pops[0] * (1.0 / 3.0) + axis_sum * (1.0 / 18.0) + diag_sum * (1.0 / 36.0)
    flow_x = diffs[1] * 2.0 + ((diffs[7] + diffs[9]) + (diffs[11] + diffs[13]))
    flow_y = diffs[3] * 2.0 + ((diffs[7] - diffs[9]) + (diffs[15] + diffs[17]))
    flow_z = diffs[5] * 2.0 + ((diffs[11] - diffs[13]) + (diffs[15] - diffs[17]))
    inverse = (1.0 / 36.0) / density
    ux, uy, uz = flow_x * inverse, flow_y * inverse, flow_z * inverse
    fluid = 1.0 - solid
    gain = density * fluid * (1.0 / relax_time)
    keep = fluid * (1.0 - 1.0 / relax_time)
    even = 0.5 * (keep + solid)
    odd = 0.5 * (keep - solid)
    rest = gain * (1.0 - 1.5 * (ux * ux + uy * uy + uz * uz))
    gain3, gain45 = gain * 3.0, gain * 4.5
    out = [None] * 19
    out[0] = (keep + solid) * pops[0] + rest
    along = {
        1: ux, 3: uy, 5: uz, 7: ux + uy, 9: ux - uy, 11: ux + uz, 13: ux - uz, 15: uy + uz, 17: uy - uz,
    }
    for i, a in along.items():
        part_even = even * sums[i] + (rest + gain45 * (a * a))
        part_odd = odd * diffs[i] + gain3 * a
        out[i] = part_even + part_odd
        out[i + 1] = part_even - part_odd
    return out


def kernel(
    sizes, off_in, frac_in, pops_in, codes_in, out_to,
    off, frac, pops, codes, out, load_sem, save_sem,
    post, s_strip, s_inner, s_end, s_col, s_corner, s_edge,
    r_inner, r_end, r_col, r_corner, r_edge, send_sem, recv_sem, relay_sem, *gathers
):
    n_gx, n_gy, n_gz, steps = sizes
    r_strip = [gathers[2 * step : 2 * step + 2] for step in range(steps)]
    layers, rows, cols = codes.shape
    length = n_gx * rows
    top = layers - 1
    gx, gy, gz = lax.axis_index("gx"), lax.axis_index("gy"), lax.axis_index("gz")
    merged = n_gz == 2
    z_moves = (1,) if merged else (1, -1)

    def peer(move):
        dx, dy, dz = move
        return (
            lax.rem(gx + (dx + n_gx), n_gx),
            lax.rem(gy + (dy + n_gy), n_gy),
            lax.rem(gz + (dz + n_gz), n_gz),
        )

    def messages(step):
        found = []
        for side, dz in ((0, 1), (1, -1)):
            for k in range(n_gx):
                found.append(
                    (
                        ("rise", "sink")[side],
                        (k, 0, dz),
                        s_strip.at[step, side],
                        lambda at, side=side: r_strip[step][side].at[
                            :, pl.ds(pl.multiple_of(at * rows, rows), rows), :
                        ],
                    )
                )
        for dx in (1, -1):
            d = side_of(dx)
            found.append(("inner", (dx, 0, 0), s_inner.at[step, d], lambda at, d=d: r_inner.at[step, d]))
            found.append(("near", (dx, 0, 0), s_end.at[step, d], lambda at, d=d: r_end.at[step, d]))
        for dy in (1, -1):
            d = side_of(dy)
            found.append(("near", (0, dy, 0), s_col.at[step, d], lambda at, d=d: r_col.at[step, d]))
        for c, (dx, dy) in enumerate(corners):
            found.append(
                ("near", (dx, dy, 0), s_corner.at[step, c], lambda at, c=c: r_corner.at[step, c])
            )
        for zi, dz in enumerate(z_moves):
            for dy in (1, -1):
                d = side_of(dy)
                for k in range(n_gx):
                    found.append(
                        (
                            "edge",
                            (k, dy, dz),
                            s_edge.at[step, d],
                            lambda at, zi=zi, d=d: r_edge.at[step, zi, d, at],
                        )
                    )
        return found

    def copy_of(step, number, entry, incoming):
        group, move, src, dst = entry
        at = lax.rem(gx - move[0] + n_gx, n_gx) if incoming else gx
        return pltpu.make_async_remote_copy(
            src_ref=src,
            dst_ref=dst(at),
            send_sem=send_sem.at[step, number],
            recv_sem=recv_sem.at[step, number],
            device_id=peer(move),
            device_id_type=MESH,
        )

    relayed = n_gx == 4
    relays = ((2, 1, 0, 3), (1, -1, 3, 1)) if relayed else ()
    strip_order = (2, 3, 1, 0) if relayed else tuple(range(n_gx))

    def strip_numbers(group):
        base = 0 if group == "rise" else n_gx
        return [base + k for k in strip_order]

    def for_strip(number, act):
        distance = number % n_gx
        if relayed and distance in (1, 3):
            pl.when(gx != (3 if distance == 1 else 0))(act)
        else:
            act()

    def start(step, group):
        entries = messages(step)
        if group in ("rise", "sink"):
            for number in strip_numbers(group):
                for_strip(number, lambda number=number: copy_of(step, number, entries[number], False).start())
            return
        for number, entry in enumerate(entries):
            if entry[0] == group:
                copy_of(step, number, entry, False).start()

    def arrive(step, group, skip=None):
        for number, entry in enumerate(messages(step)):
            if entry[0] == group and number != skip:
                copy_of(step, number, entry, True).wait_recv()

    def relay_copy(step, side, relay):
        _, move, slot, distance = relay
        block = r_strip[step][side].at[:, pl.ds(slot * rows, rows), :]
        return pltpu.make_async_remote_copy(
            src_ref=block,
            dst_ref=block,
            send_sem=relay_sem.at[step, side],
            recv_sem=recv_sem.at[step, side * n_gx + distance],
            device_id=peer((move, 0, 0)),
            device_id_type=MESH,
        )

    def forward(step, side):
        if not relayed:
            return
        number = side * n_gx + 2

        def pass_on(relay):
            copy_of(step, number, messages(step)[number], True).wait_recv()
            relay_copy(step, side, relay).start()

        for relay in relays:
            pl.when(gx == relay[0])(functools.partial(pass_on, relay))

    def arrive_rest(step, side):
        number = side * n_gx + 2 if relayed else None
        arrive(step, ("rise", "sink")[side], number)
        if relayed:
            at_end = (gx == 0) | (gx == n_gx - 1)
            pl.when(at_end)(lambda: copy_of(step, number, messages(step)[number], True).wait_recv())

    def finish(step, groups):
        entries = messages(step)
        for group in groups:
            if group in ("rise", "sink"):
                for number in strip_numbers(group):
                    for_strip(number, lambda number=number: copy_of(step, number, entries[number], False).wait_send())
                continue
            for number, entry in enumerate(entries):
                if entry[0] == group:
                    copy_of(step, number, entry, False).wait_send()

    def finish_relays(step):
        for side in (0, 1):
            for relay in relays:
                pl.when(gx == relay[0])(lambda relay=relay, side=side: relay_copy(step, side, relay).wait_send())

    inside = pl.ds(1, layers - 2)
    loads = [
        pltpu.make_async_copy(src, dst, load_sem.at[number])
        for number, (src, dst) in enumerate(
            (
                (codes_in, codes),
                (pops_in.at[:, 0], pops.at[:, 0]),
                (pops_in.at[:, top], pops.at[:, top]),
                (pops_in.at[:, inside], pops.at[:, inside]),
                (off_in, off),
                (frac_in, frac),
            )
        )
    ]
    for load in loads:
        load.start()

    moves = sorted({tuple(m % n for m, n in zip(entry[1], (n_gx, n_gy, n_gz))) for entry in messages(0)})
    barrier = pltpu.get_barrier_semaphore()
    for move in moves:
        pl.semaphore_signal(barrier, inc=1, device_id=peer(move), device_id_type=MESH)

    lane = lax.broadcasted_iota(jnp.int32, (rows, cols), 1)
    sub = lax.broadcasted_iota(jnp.int32, (rows, cols), 0)

    def to_lane(value, origin, target):
        return pltpu.roll(value, lax.rem(target - origin + 2 * cols, cols), 1)

    def publish(step, z, after, packed):
        for i in range(19):
            post[step, i, z] = after[i]
        for d in (0, 1):
            edge = rows - 1 if d == 0 else 0
            if 0 < z < top:
                target, first_row, movers = s_inner, (z - 1) * 5, x_movers[d]
            elif z == 0:
                target, first_row, movers = s_end, 0, x_bottom[d]
            else:
                target, first_row, movers = s_end, 4, x_top[d]
            for j, i in enumerate(movers):
                place = first_row + j
                target[step, d, place : place + 1, :] = after[i][edge : edge + 1, :]
        result = []
        for d in (0, 1):
            value = packed[d]
            edge = cols - 1 if d == 0 else 0
            for j, i in enumerate(y_movers[d]):
                place = j * layers + z
                value = jnp.where(lane == place, to_lane(after[i], edge, place), value)
            result.append(value)
        return tuple(result)

    def publish_strip(step, side, after):
        for j, i in enumerate((rising, sinking)[side]):
            s_strip[step, side, j] = after[i]

    def publish_edges(step, bottom_after, top_after):
        for d in (0, 1):
            dy = 1 if d == 0 else -1
            edge = cols - 1 if d == 0 else 0
            (up,) = [i for i in rising if velocities[i][1] == dy]
            (down,) = [i for i in sinking if velocities[i][1] == dy]
            place = gx * rows + sub
            spread = jnp.where(lane == place, top_after[up][:, edge : edge + 1], 0.0)
            spread = jnp.where(lane == place + length, bottom_after[down][:, edge : edge + 1], spread)
            s_edge[step, d] = jnp.sum(spread, axis=0, keepdims=True)

    def publish_columns(step, packed):
        for d in (0, 1):
            s_col[step, d] = packed[d]
        for c, (dx, dy) in enumerate(corners):
            edge = rows - 1 if dx > 0 else 0
            s_corner[step, c] = packed[side_of(dy)][edge : edge + 1, :]

    def crossing(step, side, j, i):
        dx, dy, _ = velocities[i]
        if side == 0:
            plane = gz
            near = gx * rows - dx - off[step, plane]
            far = near - 1
        else:
            plane = lax.rem(gz + 1, n_gz)
            near = gx * rows - dx + off[step, plane]
            far = near + 1
        near = lax.rem(near + 2 * length, length)
        far = lax.rem(far + 2 * length, length)
        weight = frac[step, plane].astype(jnp.float32) * (1.0 / FRAC_DEN)
        value = (1.0 - weight) * r_strip[step][side][j, pl.ds(near, rows), :]
        value = value + weight * r_strip[step][side][j, pl.ds(far, rows), :]
        if dy == 0:
            return value
        d = side_of(dy)
        zi = 0 if merged else side
        gathered = r_edge[step, zi, d, 0]
        for k in range(1, n_gx):
            gathered = gathered + r_edge[step, zi, d, k]
        place_near, place_far = near + sub, far + sub
        place_near = jnp.where(place_near >= length, place_near - length, place_near) + side * length
        place_far = jnp.where(place_far >= length, place_far - length, place_far) + side * length
        picked = jnp.where(lane == place_near, 1.0 - weight, 0.0) + jnp.where(lane == place_far, weight, 0.0)
        halo = jnp.sum(gathered * picked, axis=1, keepdims=True)
        target = 0 if dy > 0 else cols - 1
        return jnp.where(lane == target, halo, pltpu.roll(value, dy % cols, 1))

    def halo_columns(step):
        found = {}
        for dy in (1, -1):
            found[0, dy] = r_col[step, side_of(dy)]
        for c, (dx, dy) in enumerate(corners):
            edge = 0 if dx > 0 else rows - 1
            found[dx, dy] = jnp.where(
                sub == edge, r_corner[step, c], pltpu.roll(found[0, dy], dx % rows, 0)
            )
        return found

    def passed(step, z, halos, edge_layer):
        arrived = []
        for i in range(19):
            dx, dy, dz = velocities[i]
            if edge_layer == 0 and dz == 1:
                arrived.append(crossing(step, 0, rising.index(i), i))
                continue
            if edge_layer == top and dz == -1:
                arrived.append(crossing(step, 1, sinking.index(i), i))
                continue
            origin = z - dz
            value = post[step, i, origin]
            if dx:
                d = side_of(dx)
                edge = 0 if dx > 0 else rows - 1
                if 0 < origin < top:
                    row = r_inner[step, d, pl.ds((origin - 1) * 5 + x_movers[d].index(i), 1), :]
                elif origin == 0:
                    row = r_end[step, d, pl.ds(x_bottom[d].index(i), 1), :]
                else:
                    row = r_end[step, d, pl.ds(4 + x_top[d].index(i), 1), :]
                value = jnp.where(sub == edge, row, pltpu.roll(value, dx % rows, 0))
            if dy:
                target = 0 if dy > 0 else cols - 1
                place = y_movers[side_of(dy)].index(i) * layers + origin
                value = jnp.where(
                    lane == target, to_lane(halos[dx, dy], place, target), pltpu.roll(value, dy % cols, 1)
                )
            arrived.append(value)
        return arrived

    def wrap_rows(step, side):
        for j in range(5):
            r_strip[step][side][j, pl.ds(length, 2 * rows), :] = r_strip[step][side][j, pl.ds(0, 2 * rows), :]

    def inner(body, carry):
        for z in range(1, top):
            carry = body(z, carry)
        return carry

    nothing = (jnp.zeros((rows, cols), jnp.float32),) * 2

    packed = nothing
    ends = {}
    loads[0].wait()
    for number, z in ((1, 0), (2, top)):
        loads[number].wait()
        ends[z] = collide([pops[i, z] for i in range(19)], codes[z])
        packed = publish(0, z, ends[z], packed)
    publish_strip(0, 0, ends[top])
    publish_strip(0, 1, ends[0])
    publish_edges(0, ends[0], ends[top])
    pl.semaphore_wait(barrier, len(moves))
    start(0, "rise")
    start(0, "edge")
    loads[3].wait()

    def first(z, packed):
        return publish(0, z, collide([pops[i, z] for i in range(19)], codes[z]), packed)

    publish_columns(0, inner(first, packed))
    start(0, "inner")
    start(0, "near")
    finish(0, ("rise",))
    start(0, "sink")
    loads[4].wait()
    loads[5].wait()

    for step in range(1, steps):
        arrive(step - 1, "inner")
        arrive(step - 1, "near")
        halos = halo_columns(step - 1)
        forward(step - 1, 0)

        def middle(z, packed, step=step, halos=halos):
            return publish(step, z, collide(passed(step - 1, z, halos, None), codes[z]), packed)

        packed = inner(middle, nothing)
        start(step, "inner")
        forward(step - 1, 1)
        arrive(step - 1, "edge")
        arrive_rest(step - 1, 0)
        wrap_rows(step - 1, 0)
        ends[0] = collide(passed(step - 1, 0, halos, 0), codes[0])
        publish_strip(step, 1, ends[0])
        start(step, "sink")
        packed = publish(step, 0, ends[0], packed)
        arrive_rest(step - 1, 1)
        wrap_rows(step - 1, 1)
        ends[top] = collide(passed(step - 1, top, halos, top), codes[top])
        publish_strip(step, 0, ends[top])
        publish_edges(step, ends[0], ends[top])
        start(step, "edge")
        start(step, "rise")
        publish_columns(step, publish(step, top, ends[top], packed))
        start(step, "near")

    step = steps - 1
    arrive(step, "inner")
    arrive(step, "near")
    halos = halo_columns(step)
    forward(step, 1)

    def last(z, carry):
        for i, value in enumerate(passed(step, z, halos, None)):
            out[i, z] = value
        return carry

    inner(last, 0)
    saves = [pltpu.make_async_copy(out.at[:, inside], out_to.at[:, inside], save_sem.at[0])]
    saves[0].start()
    forward(step, 0)
    arrive(step, "edge")
    for side, z in ((1, top), (0, 0)):
        arrive_rest(step, side)
        wrap_rows(step, side)
        for i, value in enumerate(passed(step, z, halos, z)):
            out[i, z] = value
        saves.append(pltpu.make_async_copy(out.at[:, z], out_to.at[:, z], save_sem.at[len(saves)]))
        saves[-1].start()
    finish(0, ("sink", "inner", "near", "edge"))
    for step in range(1, steps):
        finish(step, ("rise", "sink", "inner", "near", "edge"))
    for step in range(steps):
        finish_relays(step)
    for save in saves:
        save.wait()


def hand_over(chunks, source, target, held, load_sem, save_sem):
    count = source.shape[0]
    cuts = [count * c // chunks for c in range(chunks + 1)]
    loads, saves = [], []
    for c in range(chunks):
        part = pl.ds(cuts[c], cuts[c + 1] - cuts[c])
        loads.append(pltpu.make_async_copy(source.at[part], held.at[part], load_sem.at[c]))
        saves.append(pltpu.make_async_copy(held.at[part], target.at[part], save_sem.at[c]))
    for load in loads:
        load.start()
    for load, save in zip(loads, saves):
        load.wait()
        save.start()
    for save in saves:
        save.wait()


def body(sizes, populations, solid_codes, plane_offsets, plane_fractions):
    n_gx, n_gy, n_gz = sizes
    _, layers, rows, cols = populations.shape
    steps = plane_offsets.shape[0]
    n_z = 1 if n_gz == 2 else 2
    gathered = n_gx * rows + 2 * rows
    n_messages = 2 * n_gx + 2 * 2 + 2 + 4 + n_z * 2 * n_gx
    inner_rows = -(-5 * (layers - 2) // 8) * 8
    f32 = jnp.float32
    moved = pl.pallas_call(
        functools.partial(kernel, (n_gx, n_gy, n_gz, steps)),
        out_shape=jax.ShapeDtypeStruct(populations.shape, f32),
        in_specs=[
            pl.BlockSpec(memory_space=pltpu.HBM),
            pl.BlockSpec(memory_space=pltpu.HBM),
            pl.BlockSpec(memory_space=pltpu.HBM),
            pl.BlockSpec(memory_space=pltpu.HBM),
        ],
        out_specs=pl.BlockSpec(memory_space=pltpu.HBM),
        scratch_shapes=[
            pltpu.SMEM(plane_offsets.shape, jnp.int32),
            pltpu.SMEM(plane_fractions.shape, jnp.int32),
            pltpu.VMEM(populations.shape, f32),
            pltpu.VMEM(solid_codes.shape, jnp.int32),
            pltpu.VMEM(populations.shape, f32),
            pltpu.SemaphoreType.DMA((6,)),
            pltpu.SemaphoreType.DMA((3,)),
            pltpu.VMEM((steps, 19, layers, rows, cols), f32),
            pltpu.VMEM((steps, 2, 5, rows, cols), f32),
            pltpu.VMEM((steps, 2, inner_rows, cols), f32),
            pltpu.VMEM((steps, 2, 8, cols), f32),
            pltpu.VMEM((steps, 2, rows, cols), f32),
            pltpu.VMEM((steps, 4, 1, cols), f32),
            pltpu.VMEM((steps, 2, 1, cols), f32),
            pltpu.VMEM((steps, 2, inner_rows, cols), f32),
            pltpu.VMEM((steps, 2, 8, cols), f32),
            pltpu.VMEM((steps, 2, rows, cols), f32),
            pltpu.VMEM((steps, 4, 1, cols), f32),
            pltpu.VMEM((steps, n_z, 2, n_gx, 1, cols), f32),
            pltpu.SemaphoreType.DMA((steps, n_messages)),
            pltpu.SemaphoreType.DMA((steps, n_messages)),
            pltpu.SemaphoreType.DMA((steps, 2)),
        ]
        + [pltpu.VMEM((5, gathered, cols), f32)] * (2 * steps),
        compiler_params=pltpu.CompilerParams(
            collective_id=0, has_side_effects=True, vmem_limit_bytes=60 * 1024 * 1024
        ),
    )(plane_offsets, plane_fractions, populations, solid_codes)
    chunks = 4
    return pl.pallas_call(
        functools.partial(hand_over, chunks),
        out_shape=jax.ShapeDtypeStruct(populations.shape, f32),
        in_specs=[pl.BlockSpec(memory_space=pltpu.HBM)],
        out_specs=pl.BlockSpec(memory_space=pltpu.HBM),
        scratch_shapes=[
            pltpu.VMEM(populations.shape, f32),
            pltpu.SemaphoreType.DMA((chunks,)),
            pltpu.SemaphoreType.DMA((chunks,)),
        ],
        compiler_params=pltpu.CompilerParams(vmem_limit_bytes=60 * 1024 * 1024),
    )(moved)


def solution(mesh):
    sizes = tuple(mesh.shape[name] for name in ("gx", "gy", "gz"))
    in_specs = (P(None, "gz", "gx", "gy"), P("gz", "gx", "gy"), P(), P())
    out_specs = P(None, "gz", "gx", "gy")
    return jax.shard_map(
        functools.partial(body, sizes), mesh=mesh, in_specs=in_specs, out_specs=out_specs, check_vma=False
    )
```

```python
import functools

import jax
import jax.numpy as jnp
from jax import lax
from jax.experimental import pallas as pl
from jax.experimental.pallas import tpu as pltpu
from jax.sharding import PartitionSpec as P

LEVELS = 8
FRAC_DEN = 64
MESH = pl.DeviceIdType.MESH

velocities = (
    (0, 0, 0),
    (1, 0, 0),
    (-1, 0, 0),
    (0, 1, 0),
    (0, -1, 0),
    (0, 0, 1),
    (0, 0, -1),
    (1, 1, 0),
    (-1, -1, 0),
    (1, -1, 0),
    (-1, 1, 0),
    (1, 0, 1),
    (-1, 0, -1),
    (1, 0, -1),
    (-1, 0, 1),
    (0, 1, 1),
    (0, -1, -1),
    (0, 1, -1),
    (0, -1, 1),
)
relax_time = 0.9
rising = (5, 11, 14, 15, 18)
sinking = (6, 12, 13, 16, 17)
x_movers = ((1, 7, 9, 11, 13), (2, 8, 10, 12, 14))
y_movers = ((3, 7, 10, 15, 17), (4, 8, 9, 16, 18))
x_bottom = ((1, 7, 9, 11), (2, 8, 10, 14))
x_top = ((1, 7, 9, 13), (2, 8, 10, 12))
corners = ((1, 1), (-1, -1), (1, -1), (-1, 1))


def side_of(move):
    return 0 if move > 0 else 1


def collide(pops, codes):
    solid = codes.astype(jnp.float32) * (1.0 / LEVELS)
    sums, diffs = {}, {}
    for i in range(1, 19, 2):
        sums[i] = pops[i] + pops[i + 1]
        diffs[i] = pops[i] - pops[i + 1]
    axis_sum = sums[1] + sums[3] + sums[5]
    diag_sum = (sums[7] + sums[9]) + (sums[11] + sums[13]) + (sums[15] + sums[17])
    density = pops[0] * (1.0 / 3.0) + axis_sum * (1.0 / 18.0) + diag_sum * (1.0 / 36.0)
    flow_x = diffs[1] * 2.0 + ((diffs[7] + diffs[9]) + (diffs[11] + diffs[13]))
    flow_y = diffs[3] * 2.0 + ((diffs[7] - diffs[9]) + (diffs[15] + diffs[17]))
    flow_z = diffs[5] * 2.0 + ((diffs[11] - diffs[13]) + (diffs[15] - diffs[17]))
    inverse = (1.0 / 36.0) / density
    ux, uy, uz = flow_x * inverse, flow_y * inverse, flow_z * inverse
    fluid = 1.0 - solid
    gain = density * fluid * (1.0 / relax_time)
    keep = fluid * (1.0 - 1.0 / relax_time)
    even = 0.5 * (keep + solid)
    odd = 0.5 * (keep - solid)
    rest = gain * (1.0 - 1.5 * (ux * ux + uy * uy + uz * uz))
    gain3, gain45 = gain * 3.0, gain * 4.5
    out = [None] * 19
    out[0] = (keep + solid) * pops[0] + rest
    along = {
        1: ux, 3: uy, 5: uz, 7: ux + uy, 9: ux - uy, 11: ux + uz, 13: ux - uz, 15: uy + uz, 17: uy - uz,
    }
    for i, a in along.items():
        part_even = even * sums[i] + (rest + gain45 * (a * a))
        part_odd = odd * diffs[i] + gain3 * a
        out[i] = part_even + part_odd
        out[i + 1] = part_even - part_odd
    return out


def kernel(
    sizes, off_in, frac_in, pops_in, codes_in, out_to,
    off, frac, pops, codes, out, load_sem, save_sem,
    post, s_strip, s_inner, s_end, s_col, s_corner, s_edge,
    r_inner, r_end, r_col, r_corner, r_edge, send_sem, recv_sem, *gathers
):
    n_gx, n_gy, n_gz, steps = sizes
    r_strip = [gathers[2 * step : 2 * step + 2] for step in range(steps)]
    layers, rows, cols = codes.shape
    length = n_gx * rows
    top = layers - 1
    gx, gy, gz = lax.axis_index("gx"), lax.axis_index("gy"), lax.axis_index("gz")
    merged = n_gz == 2
    z_moves = (1,) if merged else (1, -1)

    def peer(move):
        dx, dy, dz = move
        return (
            lax.rem(gx + (dx + n_gx), n_gx),
            lax.rem(gy + (dy + n_gy), n_gy),
            lax.rem(gz + (dz + n_gz), n_gz),
        )

    def messages(step):
        found = []
        for side, dz in ((0, 1), (1, -1)):
            for k in range(n_gx):
                found.append(
                    (
                        ("rise", "sink")[side],
                        (k, 0, dz),
                        s_strip.at[step, side],
                        lambda at, side=side: r_strip[step][side].at[
                            :, pl.ds(pl.multiple_of(at * rows, rows), rows), :
                        ],
                    )
                )
        for dx in (1, -1):
            d = side_of(dx)
            found.append(("inner", (dx, 0, 0), s_inner.at[step, d], lambda at, d=d: r_inner.at[step, d]))
            found.append(("near", (dx, 0, 0), s_end.at[step, d], lambda at, d=d: r_end.at[step, d]))
        for dy in (1, -1):
            d = side_of(dy)
            found.append(("near", (0, dy, 0), s_col.at[step, d], lambda at, d=d: r_col.at[step, d]))
        for c, (dx, dy) in enumerate(corners):
            found.append(
                ("near", (dx, dy, 0), s_corner.at[step, c], lambda at, c=c: r_corner.at[step, c])
            )
        for zi, dz in enumerate(z_moves):
            for dy in (1, -1):
                d = side_of(dy)
                for k in range(n_gx):
                    found.append(
                        (
                            "edge",
                            (k, dy, dz),
                            s_edge.at[step, d],
                            lambda at, zi=zi, d=d: r_edge.at[step, zi, d, at],
                        )
                    )
        return found

    def copy_of(step, number, entry, incoming):
        group, move, src, dst = entry
        at = lax.rem(gx - move[0] + n_gx, n_gx) if incoming else gx
        return pltpu.make_async_remote_copy(
            src_ref=src,
            dst_ref=dst(at),
            send_sem=send_sem.at[step, number],
            recv_sem=recv_sem.at[step, number],
            device_id=peer(move),
            device_id_type=MESH,
        )

    def start(step, group):
        for number, entry in enumerate(messages(step)):
            if entry[0] == group:
                copy_of(step, number, entry, False).start()

    def arrive(step, group):
        for number, entry in enumerate(messages(step)):
            if entry[0] == group:
                copy_of(step, number, entry, True).wait_recv()

    def finish(step, groups):
        for number, entry in enumerate(messages(step)):
            if entry[0] in groups:
                copy_of(step, number, entry, False).wait_send()

    inside = pl.ds(1, layers - 2)
    loads = [
        pltpu.make_async_copy(src, dst, load_sem.at[number])
        for number, (src, dst) in enumerate(
            (
                (codes_in, codes),
                (pops_in.at[:, 0], pops.at[:, 0]),
                (pops_in.at[:, top], pops.at[:, top]),
                (pops_in.at[:, inside], pops.at[:, inside]),
                (off_in, off),
                (frac_in, frac),
            )
        )
    ]
    for load in loads:
        load.start()

    moves = sorted({tuple(m % n for m, n in zip(entry[1], (n_gx, n_gy, n_gz))) for entry in messages(0)})
    barrier = pltpu.get_barrier_semaphore()
    for move in moves:
        pl.semaphore_signal(barrier, inc=1, device_id=peer(move), device_id_type=MESH)

    lane = lax.broadcasted_iota(jnp.int32, (rows, cols), 1)
    sub = lax.broadcasted_iota(jnp.int32, (rows, cols), 0)

    def to_lane(value, origin, target):
        return pltpu.roll(value, lax.rem(target - origin + 2 * cols, cols), 1)

    def publish(step, z, after, packed):
        for i in range(19):
            post[step, i, z] = after[i]
        for d in (0, 1):
            edge = rows - 1 if d == 0 else 0
            if 0 < z < top:
                target, first_row, movers = s_inner, (z - 1) * 5, x_movers[d]
            elif z == 0:
                target, first_row, movers = s_end, 0, x_bottom[d]
            else:
                target, first_row, movers = s_end, 4, x_top[d]
            for j, i in enumerate(movers):
                place = first_row + j
                target[step, d, place : place + 1, :] = after[i][edge : edge + 1, :]
        result = []
        for d in (0, 1):
            value = packed[d]
            edge = cols - 1 if d == 0 else 0
            for j, i in enumerate(y_movers[d]):
                place = j * layers + z
                value = jnp.where(lane == place, to_lane(after[i], edge, place), value)
            result.append(value)
        return tuple(result)

    def publish_strip(step, side, after):
        for j, i in enumerate((rising, sinking)[side]):
            s_strip[step, side, j] = after[i]

    def publish_edges(step, bottom_after, top_after):
        for d in (0, 1):
            dy = 1 if d == 0 else -1
            edge = cols - 1 if d == 0 else 0
            (up,) = [i for i in rising if velocities[i][1] == dy]
            (down,) = [i for i in sinking if velocities[i][1] == dy]
            place = gx * rows + sub
            spread = jnp.where(lane == place, top_after[up][:, edge : edge + 1], 0.0)
            spread = jnp.where(lane == place + length, bottom_after[down][:, edge : edge + 1], spread)
            s_edge[step, d] = jnp.sum(spread, axis=0, keepdims=True)

    def publish_columns(step, packed):
        for d in (0, 1):
            s_col[step, d] = packed[d]
        for c, (dx, dy) in enumerate(corners):
            edge = rows - 1 if dx > 0 else 0
            s_corner[step, c] = packed[side_of(dy)][edge : edge + 1, :]

    def crossing(step, side, j, i):
        dx, dy, _ = velocities[i]
        if side == 0:
            plane = gz
            near = gx * rows - dx - off[step, plane]
            far = near - 1
        else:
            plane = lax.rem(gz + 1, n_gz)
            near = gx * rows - dx + off[step, plane]
            far = near + 1
        near = lax.rem(near + 2 * length, length)
        far = lax.rem(far + 2 * length, length)
        weight = frac[step, plane].astype(jnp.float32) * (1.0 / FRAC_DEN)
        value = (1.0 - weight) * r_strip[step][side][j, pl.ds(near, rows), :]
        value = value + weight * r_strip[step][side][j, pl.ds(far, rows), :]
        if dy == 0:
            return value
        d = side_of(dy)
        zi = 0 if merged else side
        gathered = r_edge[step, zi, d, 0]
        for k in range(1, n_gx):
            gathered = gathered + r_edge[step, zi, d, k]
        place_near, place_far = near + sub, far + sub
        place_near = jnp.where(place_near >= length, place_near - length, place_near) + side * length
        place_far = jnp.where(place_far >= length, place_far - length, place_far) + side * length
        picked = jnp.where(lane == place_near, 1.0 - weight, 0.0) + jnp.where(lane == place_far, weight, 0.0)
        halo = jnp.sum(gathered * picked, axis=1, keepdims=True)
        target = 0 if dy > 0 else cols - 1
        return jnp.where(lane == target, halo, pltpu.roll(value, dy % cols, 1))

    def halo_columns(step):
        found = {}
        for dy in (1, -1):
            found[0, dy] = r_col[step, side_of(dy)]
        for c, (dx, dy) in enumerate(corners):
            edge = 0 if dx > 0 else rows - 1
            found[dx, dy] = jnp.where(
                sub == edge, r_corner[step, c], pltpu.roll(found[0, dy], dx % rows, 0)
            )
        return found

    def passed(step, z, halos, edge_layer):
        arrived = []
        for i in range(19):
            dx, dy, dz = velocities[i]
            if edge_layer == 0 and dz == 1:
                arrived.append(crossing(step, 0, rising.index(i), i))
                continue
            if edge_layer == top and dz == -1:
                arrived.append(crossing(step, 1, sinking.index(i), i))
                continue
            origin = z - dz
            value = post[step, i, origin]
            if dx:
                d = side_of(dx)
                edge = 0 if dx > 0 else rows - 1
                if 0 < origin < top:
                    row = r_inner[step, d, pl.ds((origin - 1) * 5 + x_movers[d].index(i), 1), :]
                elif origin == 0:
                    row = r_end[step, d, pl.ds(x_bottom[d].index(i), 1), :]
                else:
                    row = r_end[step, d, pl.ds(4 + x_top[d].index(i), 1), :]
                value = jnp.where(sub == edge, row, pltpu.roll(value, dx % rows, 0))
            if dy:
                target = 0 if dy > 0 else cols - 1
                place = y_movers[side_of(dy)].index(i) * layers + origin
                value = jnp.where(
                    lane == target, to_lane(halos[dx, dy], place, target), pltpu.roll(value, dy % cols, 1)
                )
            arrived.append(value)
        return arrived

    def wrap_rows(step, side):
        for j in range(5):
            r_strip[step][side][j, pl.ds(length, 2 * rows), :] = r_strip[step][side][j, pl.ds(0, 2 * rows), :]

    def inner(body, carry):
        for z in range(1, top):
            carry = body(z, carry)
        return carry

    nothing = (jnp.zeros((rows, cols), jnp.float32),) * 2

    packed = nothing
    ends = {}
    loads[0].wait()
    for number, z in ((1, 0), (2, top)):
        loads[number].wait()
        ends[z] = collide([pops[i, z] for i in range(19)], codes[z])
        packed = publish(0, z, ends[z], packed)
    publish_strip(0, 0, ends[top])
    publish_strip(0, 1, ends[0])
    publish_edges(0, ends[0], ends[top])
    pl.semaphore_wait(barrier, len(moves))
    start(0, "rise")
    loads[3].wait()

    def first(z, packed):
        return publish(0, z, collide([pops[i, z] for i in range(19)], codes[z]), packed)

    publish_columns(0, inner(first, packed))
    start(0, "inner")
    start(0, "near")
    start(0, "edge")
    finish(0, ("rise",))
    start(0, "sink")
    loads[4].wait()
    loads[5].wait()

    for step in range(1, steps):
        arrive(step - 1, "inner")
        arrive(step - 1, "near")
        halos = halo_columns(step - 1)

        def middle(z, packed, step=step, halos=halos):
            return publish(step, z, collide(passed(step - 1, z, halos, None), codes[z]), packed)

        packed = inner(middle, nothing)
        start(step, "inner")
        arrive(step - 1, "edge")
        arrive(step - 1, "rise")
        wrap_rows(step - 1, 0)
        ends[0] = collide(passed(step - 1, 0, halos, 0), codes[0])
        publish_strip(step, 1, ends[0])
        start(step, "sink")
        packed = publish(step, 0, ends[0], packed)
        arrive(step - 1, "sink")
        wrap_rows(step - 1, 1)
        ends[top] = collide(passed(step - 1, top, halos, top), codes[top])
        publish_strip(step, 0, ends[top])
        start(step, "rise")
        publish_columns(step, publish(step, top, ends[top], packed))
        start(step, "near")
        publish_edges(step, ends[0], ends[top])
        start(step, "edge")

    step = steps - 1
    arrive(step, "inner")
    arrive(step, "near")
    halos = halo_columns(step)

    def last(z, carry):
        for i, value in enumerate(passed(step, z, halos, None)):
            out[i, z] = value
        return carry

    inner(last, 0)
    saves = [pltpu.make_async_copy(out.at[:, inside], out_to.at[:, inside], save_sem.at[0])]
    saves[0].start()
    arrive(step, "edge")
    for side, z in ((1, top), (0, 0)):
        arrive(step, ("rise", "sink")[side])
        wrap_rows(step, side)
        for i, value in enumerate(passed(step, z, halos, z)):
            out[i, z] = value
        saves.append(pltpu.make_async_copy(out.at[:, z], out_to.at[:, z], save_sem.at[len(saves)]))
        saves[-1].start()
    finish(0, ("sink", "inner", "near", "edge"))
    for step in range(1, steps):
        finish(step, ("rise", "sink", "inner", "near", "edge"))
    for save in saves:
        save.wait()


def hand_over(chunks, source, target, held, load_sem, save_sem):
    count = source.shape[0]
    cuts = [count * c // chunks for c in range(chunks + 1)]
    loads, saves = [], []
    for c in range(chunks):
        part = pl.ds(cuts[c], cuts[c + 1] - cuts[c])
        loads.append(pltpu.make_async_copy(source.at[part], held.at[part], load_sem.at[c]))
        saves.append(pltpu.make_async_copy(held.at[part], target.at[part], save_sem.at[c]))
    for load in loads:
        load.start()
    for load, save in zip(loads, saves):
        load.wait()
        save.start()
    for save in saves:
        save.wait()


def body(sizes, populations, solid_codes, plane_offsets, plane_fractions):
    n_gx, n_gy, n_gz = sizes
    _, layers, rows, cols = populations.shape
    steps = plane_offsets.shape[0]
    n_z = 1 if n_gz == 2 else 2
    gathered = n_gx * rows + 2 * rows
    n_messages = 2 * n_gx + 2 * 2 + 2 + 4 + n_z * 2 * n_gx
    inner_rows = -(-5 * (layers - 2) // 8) * 8
    f32 = jnp.float32
    moved = pl.pallas_call(
        functools.partial(kernel, (n_gx, n_gy, n_gz, steps)),
        out_shape=jax.ShapeDtypeStruct(populations.shape, f32),
        in_specs=[
            pl.BlockSpec(memory_space=pltpu.HBM),
            pl.BlockSpec(memory_space=pltpu.HBM),
            pl.BlockSpec(memory_space=pltpu.HBM),
            pl.BlockSpec(memory_space=pltpu.HBM),
        ],
        out_specs=pl.BlockSpec(memory_space=pltpu.HBM),
        scratch_shapes=[
            pltpu.SMEM(plane_offsets.shape, jnp.int32),
            pltpu.SMEM(plane_fractions.shape, jnp.int32),
            pltpu.VMEM(populations.shape, f32),
            pltpu.VMEM(solid_codes.shape, jnp.int32),
            pltpu.VMEM(populations.shape, f32),
            pltpu.SemaphoreType.DMA((6,)),
            pltpu.SemaphoreType.DMA((3,)),
            pltpu.VMEM((steps, 19, layers, rows, cols), f32),
            pltpu.VMEM((steps, 2, 5, rows, cols), f32),
            pltpu.VMEM((steps, 2, inner_rows, cols), f32),
            pltpu.VMEM((steps, 2, 8, cols), f32),
            pltpu.VMEM((steps, 2, rows, cols), f32),
            pltpu.VMEM((steps, 4, 1, cols), f32),
            pltpu.VMEM((steps, 2, 1, cols), f32),
            pltpu.VMEM((steps, 2, inner_rows, cols), f32),
            pltpu.VMEM((steps, 2, 8, cols), f32),
            pltpu.VMEM((steps, 2, rows, cols), f32),
            pltpu.VMEM((steps, 4, 1, cols), f32),
            pltpu.VMEM((steps, n_z, 2, n_gx, 1, cols), f32),
            pltpu.SemaphoreType.DMA((steps, n_messages)),
            pltpu.SemaphoreType.DMA((steps, n_messages)),
        ]
        + [pltpu.VMEM((5, gathered, cols), f32)] * (2 * steps),
        compiler_params=pltpu.CompilerParams(
            collective_id=0, has_side_effects=True, vmem_limit_bytes=60 * 1024 * 1024
        ),
    )(plane_offsets, plane_fractions, populations, solid_codes)
    chunks = 10
    return pl.pallas_call(
        functools.partial(hand_over, chunks),
        out_shape=jax.ShapeDtypeStruct(populations.shape, f32),
        in_specs=[pl.BlockSpec(memory_space=pltpu.HBM)],
        out_specs=pl.BlockSpec(memory_space=pltpu.HBM),
        scratch_shapes=[
            pltpu.VMEM(populations.shape, f32),
            pltpu.SemaphoreType.DMA((chunks,)),
            pltpu.SemaphoreType.DMA((chunks,)),
        ],
        compiler_params=pltpu.CompilerParams(vmem_limit_bytes=60 * 1024 * 1024),
    )(moved)


def solution(mesh):
    sizes = tuple(mesh.shape[name] for name in ("gx", "gy", "gz"))
    in_specs = (P(None, "gz", "gx", "gy"), P("gz", "gx", "gy"), P(), P())
    out_specs = P(None, "gz", "gx", "gy")
    return jax.shard_map(
        functools.partial(body, sizes), mesh=mesh, in_specs=in_specs, out_specs=out_specs, check_vma=False
    )
```

```python
import functools

import jax
import jax.numpy as jnp
from jax import lax
from jax.experimental import pallas as pl
from jax.experimental.pallas import tpu as pltpu
from jax.sharding import PartitionSpec as P

LEVELS = 8
FRAC_DEN = 64
MESH = pl.DeviceIdType.MESH

velocities = (
    (0, 0, 0),
    (1, 0, 0),
    (-1, 0, 0),
    (0, 1, 0),
    (0, -1, 0),
    (0, 0, 1),
    (0, 0, -1),
    (1, 1, 0),
    (-1, -1, 0),
    (1, -1, 0),
    (-1, 1, 0),
    (1, 0, 1),
    (-1, 0, -1),
    (1, 0, -1),
    (-1, 0, 1),
    (0, 1, 1),
    (0, -1, -1),
    (0, 1, -1),
    (0, -1, 1),
)
relax_time = 0.9
rising = (5, 11, 14, 15, 18)
sinking = (6, 12, 13, 16, 17)
x_movers = ((1, 7, 9, 11, 13), (2, 8, 10, 12, 14))
y_movers = ((3, 7, 10, 15, 17), (4, 8, 9, 16, 18))
x_bottom = ((1, 7, 9, 11), (2, 8, 10, 14))
x_top = ((1, 7, 9, 13), (2, 8, 10, 12))
corners = ((1, 1), (-1, -1), (1, -1), (-1, 1))


def side_of(move):
    return 0 if move > 0 else 1


def collide(pops, codes):
    solid = codes.astype(jnp.float32) * (1.0 / LEVELS)
    sums, diffs = {}, {}
    for i in range(1, 19, 2):
        sums[i] = pops[i] + pops[i + 1]
        diffs[i] = pops[i] - pops[i + 1]
    axis_sum = sums[1] + sums[3] + sums[5]
    diag_sum = (sums[7] + sums[9]) + (sums[11] + sums[13]) + (sums[15] + sums[17])
    density = pops[0] * (1.0 / 3.0) + axis_sum * (1.0 / 18.0) + diag_sum * (1.0 / 36.0)
    flow_x = diffs[1] * 2.0 + ((diffs[7] + diffs[9]) + (diffs[11] + diffs[13]))
    flow_y = diffs[3] * 2.0 + ((diffs[7] - diffs[9]) + (diffs[15] + diffs[17]))
    flow_z = diffs[5] * 2.0 + ((diffs[11] - diffs[13]) + (diffs[15] - diffs[17]))
    inverse = (1.0 / 36.0) / density
    ux, uy, uz = flow_x * inverse, flow_y * inverse, flow_z * inverse
    fluid = 1.0 - solid
    gain = density * fluid * (1.0 / relax_time)
    keep = fluid * (1.0 - 1.0 / relax_time)
    even = 0.5 * (keep + solid)
    odd = 0.5 * (keep - solid)
    rest = gain * (1.0 - 1.5 * (ux * ux + uy * uy + uz * uz))
    gain3, gain45 = gain * 3.0, gain * 4.5
    out = [None] * 19
    out[0] = (keep + solid) * pops[0] + rest
    along = {
        1: ux, 3: uy, 5: uz, 7: ux + uy, 9: ux - uy, 11: ux + uz, 13: ux - uz, 15: uy + uz, 17: uy - uz,
    }
    for i, a in along.items():
        part_even = even * sums[i] + (rest + gain45 * (a * a))
        part_odd = odd * diffs[i] + gain3 * a
        out[i] = part_even + part_odd
        out[i + 1] = part_even - part_odd
    return out


def kernel(
    sizes, off_in, frac_in, pops_in, codes_in, out_to,
    off, frac, pops, codes, out, load_sem, save_sem,
    post, s_strip, s_inner, s_end, s_col, s_corner, s_edge,
    r_inner, r_end, r_col, r_corner, r_edge, send_sem, recv_sem, *gathers
):
    n_gx, n_gy, n_gz, steps = sizes
    r_strip = [gathers[2 * step : 2 * step + 2] for step in range(steps)]
    layers, rows, cols = codes.shape
    length = n_gx * rows
    top = layers - 1
    gx, gy, gz = lax.axis_index("gx"), lax.axis_index("gy"), lax.axis_index("gz")
    merged = n_gz == 2
    z_moves = (1,) if merged else (1, -1)

    def peer(move):
        dx, dy, dz = move
        return (
            lax.rem(gx + (dx + n_gx), n_gx),
            lax.rem(gy + (dy + n_gy), n_gy),
            lax.rem(gz + (dz + n_gz), n_gz),
        )

    def messages(step):
        found = []
        for side, dz in ((0, 1), (1, -1)):
            for k in range(n_gx):
                found.append(
                    (
                        ("rise", "sink")[side],
                        (k, 0, dz),
                        s_strip.at[step, side],
                        lambda at, side=side: r_strip[step][side].at[
                            :, pl.ds(pl.multiple_of(at * rows, rows), rows), :
                        ],
                    )
                )
        for dx in (1, -1):
            d = side_of(dx)
            found.append(("inner", (dx, 0, 0), s_inner.at[step, d], lambda at, d=d: r_inner.at[step, d]))
            found.append(("near", (dx, 0, 0), s_end.at[step, d], lambda at, d=d: r_end.at[step, d]))
        for dy in (1, -1):
            d = side_of(dy)
            found.append(("near", (0, dy, 0), s_col.at[step, d], lambda at, d=d: r_col.at[step, d]))
        for c, (dx, dy) in enumerate(corners):
            found.append(
                ("near", (dx, dy, 0), s_corner.at[step, c], lambda at, c=c: r_corner.at[step, c])
            )
        for zi, dz in enumerate(z_moves):
            for dy in (1, -1):
                d = side_of(dy)
                for k in range(n_gx):
                    found.append(
                        (
                            "edge",
                            (k, dy, dz),
                            s_edge.at[step, d],
                            lambda at, zi=zi, d=d: r_edge.at[step, zi, d, at],
                        )
                    )
        return found

    def copy_of(step, number, entry, incoming):
        group, move, src, dst = entry
        at = lax.rem(gx - move[0] + n_gx, n_gx) if incoming else gx
        return pltpu.make_async_remote_copy(
            src_ref=src,
            dst_ref=dst(at),
            send_sem=send_sem.at[step, number],
            recv_sem=recv_sem.at[step, number],
            device_id=peer(move),
            device_id_type=MESH,
        )

    def start(step, group):
        for number, entry in enumerate(messages(step)):
            if entry[0] == group:
                copy_of(step, number, entry, False).start()

    def arrive(step, group):
        for number, entry in enumerate(messages(step)):
            if entry[0] == group:
                copy_of(step, number, entry, True).wait_recv()

    def finish(step, groups):
        for number, entry in enumerate(messages(step)):
            if entry[0] in groups:
                copy_of(step, number, entry, False).wait_send()

    inside = pl.ds(1, layers - 2)
    loads = [
        pltpu.make_async_copy(src, dst, load_sem.at[number])
        for number, (src, dst) in enumerate(
            (
                (codes_in, codes),
                (pops_in.at[:, 0], pops.at[:, 0]),
                (pops_in.at[:, top], pops.at[:, top]),
                (pops_in.at[:, inside], pops.at[:, inside]),
                (off_in, off),
                (frac_in, frac),
            )
        )
    ]
    for load in loads:
        load.start()

    moves = sorted({tuple(m % n for m, n in zip(entry[1], (n_gx, n_gy, n_gz))) for entry in messages(0)})
    barrier = pltpu.get_barrier_semaphore()
    for move in moves:
        pl.semaphore_signal(barrier, inc=1, device_id=peer(move), device_id_type=MESH)

    lane = lax.broadcasted_iota(jnp.int32, (rows, cols), 1)
    sub = lax.broadcasted_iota(jnp.int32, (rows, cols), 0)

    def to_lane(value, origin, target):
        return pltpu.roll(value, lax.rem(target - origin + 2 * cols, cols), 1)

    def publish(step, z, after, packed):
        for i in range(19):
            post[step, i, z] = after[i]
        for d in (0, 1):
            edge = rows - 1 if d == 0 else 0
            if 0 < z < top:
                target, first_row, movers = s_inner, (z - 1) * 5, x_movers[d]
            elif z == 0:
                target, first_row, movers = s_end, 0, x_bottom[d]
            else:
                target, first_row, movers = s_end, 4, x_top[d]
            for j, i in enumerate(movers):
                place = first_row + j
                target[step, d, place : place + 1, :] = after[i][edge : edge + 1, :]
        result = []
        for d in (0, 1):
            value = packed[d]
            edge = cols - 1 if d == 0 else 0
            for j, i in enumerate(y_movers[d]):
                place = j * layers + z
                value = jnp.where(lane == place, to_lane(after[i], edge, place), value)
            result.append(value)
        return tuple(result)

    def publish_strip(step, side, after):
        for j, i in enumerate((rising, sinking)[side]):
            s_strip[step, side, j] = after[i]

    def publish_edges(step, bottom_after, top_after):
        for d in (0, 1):
            dy = 1 if d == 0 else -1
            edge = cols - 1 if d == 0 else 0
            (up,) = [i for i in rising if velocities[i][1] == dy]
            (down,) = [i for i in sinking if velocities[i][1] == dy]
            place = gx * rows + sub
            spread = jnp.where(lane == place, top_after[up][:, edge : edge + 1], 0.0)
            spread = jnp.where(lane == place + length, bottom_after[down][:, edge : edge + 1], spread)
            s_edge[step, d] = jnp.sum(spread, axis=0, keepdims=True)

    def publish_columns(step, packed):
        for d in (0, 1):
            s_col[step, d] = packed[d]
        for c, (dx, dy) in enumerate(corners):
            edge = rows - 1 if dx > 0 else 0
            s_corner[step, c] = packed[side_of(dy)][edge : edge + 1, :]

    def crossing(step, side, j, i):
        dx, dy, _ = velocities[i]
        if side == 0:
            plane = gz
            near = gx * rows - dx - off[step, plane]
            far = near - 1
        else:
            plane = lax.rem(gz + 1, n_gz)
            near = gx * rows - dx + off[step, plane]
            far = near + 1
        near = lax.rem(near + 2 * length, length)
        far = lax.rem(far + 2 * length, length)
        weight = frac[step, plane].astype(jnp.float32) * (1.0 / FRAC_DEN)
        value = (1.0 - weight) * r_strip[step][side][j, pl.ds(near, rows), :]
        value = value + weight * r_strip[step][side][j, pl.ds(far, rows), :]
        if dy == 0:
            return value
        d = side_of(dy)
        zi = 0 if merged else side
        gathered = r_edge[step, zi, d, 0]
        for k in range(1, n_gx):
            gathered = gathered + r_edge[step, zi, d, k]
        place_near, place_far = near + sub, far + sub
        place_near = jnp.where(place_near >= length, place_near - length, place_near) + side * length
        place_far = jnp.where(place_far >= length, place_far - length, place_far) + side * length
        picked = jnp.where(lane == place_near, 1.0 - weight, 0.0) + jnp.where(lane == place_far, weight, 0.0)
        halo = jnp.sum(gathered * picked, axis=1, keepdims=True)
        target = 0 if dy > 0 else cols - 1
        return jnp.where(lane == target, halo, pltpu.roll(value, dy % cols, 1))

    def halo_columns(step):
        found = {}
        for dy in (1, -1):
            found[0, dy] = r_col[step, side_of(dy)]
        for c, (dx, dy) in enumerate(corners):
            edge = 0 if dx > 0 else rows - 1
            found[dx, dy] = jnp.where(
                sub == edge, r_corner[step, c], pltpu.roll(found[0, dy], dx % rows, 0)
            )
        return found

    def passed(step, z, halos, edge_layer):
        arrived = []
        for i in range(19):
            dx, dy, dz = velocities[i]
            if edge_layer == 0 and dz == 1:
                arrived.append(crossing(step, 0, rising.index(i), i))
                continue
            if edge_layer == top and dz == -1:
                arrived.append(crossing(step, 1, sinking.index(i), i))
                continue
            origin = z - dz
            value = post[step, i, origin]
            if dx:
                d = side_of(dx)
                edge = 0 if dx > 0 else rows - 1
                if 0 < origin < top:
                    row = r_inner[step, d, pl.ds((origin - 1) * 5 + x_movers[d].index(i), 1), :]
                elif origin == 0:
                    row = r_end[step, d, pl.ds(x_bottom[d].index(i), 1), :]
                else:
                    row = r_end[step, d, pl.ds(4 + x_top[d].index(i), 1), :]
                value = jnp.where(sub == edge, row, pltpu.roll(value, dx % rows, 0))
            if dy:
                target = 0 if dy > 0 else cols - 1
                place = y_movers[side_of(dy)].index(i) * layers + origin
                value = jnp.where(
                    lane == target, to_lane(halos[dx, dy], place, target), pltpu.roll(value, dy % cols, 1)
                )
            arrived.append(value)
        return arrived

    def wrap_rows(step, side):
        for j in range(5):
            r_strip[step][side][j, pl.ds(length, 2 * rows), :] = r_strip[step][side][j, pl.ds(0, 2 * rows), :]

    def inner(body, carry):
        for z in range(1, top):
            carry = body(z, carry)
        return carry

    nothing = (jnp.zeros((rows, cols), jnp.float32),) * 2

    packed = nothing
    ends = {}
    loads[0].wait()
    for number, z in ((1, 0), (2, top)):
        loads[number].wait()
        ends[z] = collide([pops[i, z] for i in range(19)], codes[z])
        packed = publish(0, z, ends[z], packed)
    publish_strip(0, 0, ends[top])
    publish_strip(0, 1, ends[0])
    publish_edges(0, ends[0], ends[top])
    pl.semaphore_wait(barrier, len(moves))
    start(0, "edge")
    start(0, "rise")
    start(0, "sink")
    loads[3].wait()

    def first(z, packed):
        return publish(0, z, collide([pops[i, z] for i in range(19)], codes[z]), packed)

    publish_columns(0, inner(first, packed))
    start(0, "near")
    start(0, "inner")
    loads[4].wait()
    loads[5].wait()

    for step in range(1, steps):
        arrive(step - 1, "inner")
        arrive(step - 1, "near")
        halos = halo_columns(step - 1)

        def middle(z, packed, step=step, halos=halos):
            return publish(step, z, collide(passed(step - 1, z, halos, None), codes[z]), packed)

        packed = inner(middle, nothing)
        start(step, "inner")
        arrive(step - 1, "edge")
        arrive(step - 1, "rise")
        wrap_rows(step - 1, 0)
        ends[0] = collide(passed(step - 1, 0, halos, 0), codes[0])
        publish_strip(step, 1, ends[0])
        start(step, "sink")
        packed = publish(step, 0, ends[0], packed)
        arrive(step - 1, "sink")
        wrap_rows(step - 1, 1)
        ends[top] = collide(passed(step - 1, top, halos, top), codes[top])
        publish_strip(step, 0, ends[top])
        publish_edges(step, ends[0], ends[top])
        start(step, "edge")
        start(step, "rise")
        publish_columns(step, publish(step, top, ends[top], packed))
        start(step, "near")

    step = steps - 1
    arrive(step, "inner")
    arrive(step, "near")
    halos = halo_columns(step)

    def last(z, carry):
        for i, value in enumerate(passed(step, z, halos, None)):
            out[i, z] = value
        return carry

    inner(last, 0)
    saves = [pltpu.make_async_copy(out.at[:, inside], out_to.at[:, inside], save_sem.at[0])]
    saves[0].start()
    arrive(step, "edge")
    for side, z in ((1, top), (0, 0)):
        arrive(step, ("rise", "sink")[side])
        wrap_rows(step, side)
        for i, value in enumerate(passed(step, z, halos, z)):
            out[i, z] = value
        saves.append(pltpu.make_async_copy(out.at[:, z], out_to.at[:, z], save_sem.at[len(saves)]))
        saves[-1].start()
    for step in range(steps):
        finish(step, ("rise", "sink", "inner", "near", "edge"))
    for save in saves:
        save.wait()


def hand_over(chunks, source, target, held, load_sem, save_sem):
    count = source.shape[0]
    cuts = [count * c // chunks for c in range(chunks + 1)]
    loads, saves = [], []
    for c in range(chunks):
        part = pl.ds(cuts[c], cuts[c + 1] - cuts[c])
        loads.append(pltpu.make_async_copy(source.at[part], held.at[part], load_sem.at[c]))
        saves.append(pltpu.make_async_copy(held.at[part], target.at[part], save_sem.at[c]))
    for load in loads:
        load.start()
    for load, save in zip(loads, saves):
        load.wait()
        save.start()
    for save in saves:
        save.wait()


def body(sizes, populations, solid_codes, plane_offsets, plane_fractions):
    n_gx, n_gy, n_gz = sizes
    _, layers, rows, cols = populations.shape
    steps = plane_offsets.shape[0]
    n_z = 1 if n_gz == 2 else 2
    gathered = n_gx * rows + 2 * rows
    n_messages = 2 * n_gx + 2 * 2 + 2 + 4 + n_z * 2 * n_gx
    inner_rows = -(-5 * (layers - 2) // 8) * 8
    f32 = jnp.float32
    moved = pl.pallas_call(
        functools.partial(kernel, (n_gx, n_gy, n_gz, steps)),
        out_shape=jax.ShapeDtypeStruct(populations.shape, f32),
        in_specs=[
            pl.BlockSpec(memory_space=pltpu.HBM),
            pl.BlockSpec(memory_space=pltpu.HBM),
            pl.BlockSpec(memory_space=pltpu.HBM),
            pl.BlockSpec(memory_space=pltpu.HBM),
        ],
        out_specs=pl.BlockSpec(memory_space=pltpu.HBM),
        scratch_shapes=[
            pltpu.SMEM(plane_offsets.shape, jnp.int32),
            pltpu.SMEM(plane_fractions.shape, jnp.int32),
            pltpu.VMEM(populations.shape, f32),
            pltpu.VMEM(solid_codes.shape, jnp.int32),
            pltpu.VMEM(populations.shape, f32),
            pltpu.SemaphoreType.DMA((6,)),
            pltpu.SemaphoreType.DMA((3,)),
            pltpu.VMEM((steps, 19, layers, rows, cols), f32),
            pltpu.VMEM((steps, 2, 5, rows, cols), f32),
            pltpu.VMEM((steps, 2, inner_rows, cols), f32),
            pltpu.VMEM((steps, 2, 8, cols), f32),
            pltpu.VMEM((steps, 2, rows, cols), f32),
            pltpu.VMEM((steps, 4, 1, cols), f32),
            pltpu.VMEM((steps, 2, 1, cols), f32),
            pltpu.VMEM((steps, 2, inner_rows, cols), f32),
            pltpu.VMEM((steps, 2, 8, cols), f32),
            pltpu.VMEM((steps, 2, rows, cols), f32),
            pltpu.VMEM((steps, 4, 1, cols), f32),
            pltpu.VMEM((steps, n_z, 2, n_gx, 1, cols), f32),
            pltpu.SemaphoreType.DMA((steps, n_messages)),
            pltpu.SemaphoreType.DMA((steps, n_messages)),
        ]
        + [pltpu.VMEM((5, gathered, cols), f32)] * (2 * steps),
        compiler_params=pltpu.CompilerParams(
            collective_id=0, has_side_effects=True, vmem_limit_bytes=60 * 1024 * 1024
        ),
    )(plane_offsets, plane_fractions, populations, solid_codes)
    chunks = 4
    return pl.pallas_call(
        functools.partial(hand_over, chunks),
        out_shape=jax.ShapeDtypeStruct(populations.shape, f32),
        in_specs=[pl.BlockSpec(memory_space=pltpu.HBM)],
        out_specs=pl.BlockSpec(memory_space=pltpu.HBM),
        scratch_shapes=[
            pltpu.VMEM(populations.shape, f32),
            pltpu.SemaphoreType.DMA((chunks,)),
            pltpu.SemaphoreType.DMA((chunks,)),
        ],
        compiler_params=pltpu.CompilerParams(vmem_limit_bytes=60 * 1024 * 1024),
    )(moved)


def solution(mesh):
    sizes = tuple(mesh.shape[name] for name in ("gx", "gy", "gz"))
    in_specs = (P(None, "gz", "gx", "gy"), P("gz", "gx", "gy"), P(), P())
    out_specs = P(None, "gz", "gx", "gy")
    return jax.shard_map(
        functools.partial(body, sizes), mesh=mesh, in_specs=in_specs, out_specs=out_specs, check_vma=False
    )
```
